32 devices in a mesh: grp: 2 (over y), visit: 16 (over z, x, core).
Axes of the slice: x: 2, y: 2, z: 4, core: 2. Of those that a mesh axis runs over, the one named last changes fastest.
Arguments:
- science: float32 [8192, 1024], P(('grp', 'visit')), parts along dimension 0, may hold values from -6 to 6
- patches: float32 [256, 256, 256], P(('grp', 'visit')), parts along dimension 0, may hold values from -6 to 6
- margin: int32 [128, 3], P('grp'), parts along dimension 0, may hold values from 0 to 255, as said below
- kernel_coef: float32 [27, 128], P(None, ('grp', 'visit')), parts along dimension 1, may hold values from -4 to 4
- ccd_first: int32 [32], P('grp'), parts along dimension 0, may hold values 0 or 1
Outputs:
- patch_mean: float32 [256, 256, 256], P(('grp', 'visit')), parts along dimension 0
The draws below stay inside these ranges and needn't reach their ends.
There are 2 independent parts, one for each index of `grp`. The reference program is written for one: setup_inputs(seed, part) draws one part's arguments, and reference() takes and returns one part's arrays. A program takes and returns all parts, laid end to end along the dimension named above; each array names one. Nothing has to cross between parts.
Inputs may be any that keep to these rules, and one draw needn't show every extreme that they name: `margin`: column 0 is a patch id, columns 1 and 2 are offsets below 256. A tile of strip d names a patch owned by strip d - 1, d or d + 1. Among the 4 tiles of one strip at most 2 name patches of one owner (patch id // 8), and in every strip some owner is named exactly 2 times.
All inputs are finite; a program needn't handle non-finite values.
Results may differ from the reference program's by a relative error of at most 0.004.
Values may be sent and summed in bfloat16 or wider, within the bound.
A program may use at most 64 MiB of HBM per device.

```python
import jax
import jax.numpy as jnp
from jax import lax

TILE = 256
RADIUS = 10
SIGMAS = 3
ORDERS = 3
NBASIS = 27
TILES_DEV = 4
PATCH_DEV = 8
OWNERS = 16
CAP = 2
TILES = 64
PATCHES = 128
ROWS = 4096
STRIP = 1024


def draw_margin(key, part):
    keys = jax.random.split(key, 6)
    strips = jnp.arange(OWNERS)
    first_pick = jax.random.randint(keys[0], (OWNERS,), 0, 3) - 1
    end_pick = jax.random.randint(keys[1], (OWNERS,), 0, 2)
    favored = jnp.where(strips == 0, end_pick, jnp.where(strips == OWNERS - 1, end_pick - 1, first_pick))
    pick_other = jax.random.randint(keys[2], (OWNERS, TILES_DEV), 0, 2)
    lower_other = jnp.where(favored == -1, 0, -1)
    upper_other = jnp.where(favored == 1, 0, 1)
    middle_other = jnp.where(pick_other == 0, lower_other[:, None], upper_other[:, None])
    end_other = jnp.where(strips == 0, 1 - favored, -1 - favored)
    at_end = (strips == 0) | (strips == OWNERS - 1)
    other = jnp.where(at_end[:, None], end_other[:, None], middle_other)
    positions = jnp.arange(TILES_DEV)
    offset_grid = jnp.where(positions[None, :] < CAP, favored[:, None], other)
    shuffle_keys = jax.random.randint(keys[3], (OWNERS, TILES_DEV), 0, 1048576) * TILES_DEV + positions[None, :]
    order = jnp.argsort(shuffle_keys, axis=1)
    offset_grid = jnp.take_along_axis(offset_grid, order, axis=1)
    owners_drawn = strips[:, None] + offset_grid
    local_patch = jax.random.randint(keys[4], (OWNERS, TILES_DEV), 0, PATCH_DEV)
    patch_ids = (owners_drawn * PATCH_DEV + local_patch).reshape(TILES, 1)
    offsets = jax.random.randint(keys[5], (TILES, 2), 0, TILE)
    return jnp.concatenate([patch_ids, offsets], axis=1).astype(jnp.int32)


def with_ends(entries, key, smallest, largest):
    extent = entries.shape
    spot = [jax.random.randint(jax.random.fold_in(key, axis), (), 0, extent[axis]) for axis in range(len(extent))]
    entries = entries.at[tuple(spot)].set(smallest)
    longest = extent.index(max(extent))
    spot[longest] = (spot[longest] + 1) % extent[longest]
    return entries.at[tuple(spot)].set(largest)


def levels(stream_key, shape, cuts, least, top_value):
    level, own = 1.0, jax.random.fold_in(stream_key, 6)
    for axis_at, blocks in cuts:
        draws = jnp.exp(jax.random.uniform(jax.random.fold_in(own, axis_at), (blocks,), jnp.float32, least / len(cuts), top_value / len(cuts)))
        level = level * jnp.repeat(draws, shape[axis_at] // blocks).reshape([-1 if axis == axis_at else 1 for axis in range(len(shape))])
    return level


def scatter_about(stream_key, extent, scale, reach, cuts=(), dtype=jnp.bfloat16):
    factor_of = levels(stream_key, extent, cuts, -0.22, 0.18) if cuts else 1.0
    array = jax.random.normal(stream_key, extent, jnp.float32) * scale * factor_of
    return jnp.minimum(jnp.maximum(array, -reach), reach).astype(dtype)


def setup_inputs(seed: int = 0, part: int = 0) -> dict:
    splits = jax.random.split(jax.random.key(seed), 6)
    part_splits = jax.random.split(jax.random.fold_in(splits[5], part), 6)
    science = scatter_about(part_splits[0], (ROWS, STRIP), 1.0, 6.0, ((0, 16),), jnp.float32)
    patches = scatter_about(part_splits[1], (PATCHES, TILE, TILE), 1.0, 6.0, ((0, 16),), jnp.float32)
    margin = draw_margin(jax.random.fold_in(jax.random.fold_in(splits[5], part), 71), part)
    kernel_coef = scatter_about(part_splits[3], (NBASIS, TILES), 1.0, 4.0, ((1, 16),), jnp.float32)
    ccd_first = with_ends((jax.random.randint(part_splits[4], (OWNERS,), 0, 4) < 1).astype(jnp.int32), jax.random.fold_in(part_splits[4], 1), 0, 1)
    return {"science": science, "patches": patches, "margin": margin, "kernel_coef": kernel_coef, "ccd_first": ccd_first}


def basis_table():
    width = TILE + 2 * RADIUS
    offsets = (jnp.arange(width)[None, :] - jnp.arange(TILE)[:, None] - RADIUS).astype(jnp.float32)
    inside = jnp.abs(offsets) <= RADIUS
    taps = jnp.arange(-RADIUS, RADIUS + 1).astype(jnp.float32)
    tables = []
    for sigma_index in range(SIGMAS):
        sigma = 0.75 * 2.0 ** sigma_index
        normal_sum = jnp.sum(jnp.exp(-taps * taps / (2.0 * sigma * sigma)))
        profile = jnp.where(inside, jnp.exp(-offsets * offsets / (2.0 * sigma * sigma)) / normal_sum, 0.0)
        tables.append(jnp.stack([profile * (offsets / sigma) ** order_index for order_index in range(ORDERS)]))
    return jnp.stack(tables)


def shift_tiles(stack, down, right):
    span = stack.shape[1]
    positions = jnp.arange(span)
    row_source = (positions[None, :] - down[:, None]) % span
    moved = jnp.take_along_axis(stack, row_source[:, :, None], axis=1)
    col_source = (positions[None, :] - right[:, None]) % span
    return jnp.take_along_axis(moved, col_source[:, None, :], axis=2)


def match_strip(extended, science_strip, weights):
    table = basis_table()
    width = TILE + 2 * RADIUS
    starts = jnp.arange(TILES_DEV)[:, None] * TILE + jnp.arange(width)[None, :]
    windows = jnp.take(extended, starts, axis=1)
    mixing = weights.reshape(SIGMAS, ORDERS, ORDERS, TILES_DEV)
    mixed = jnp.einsum('spqt,sqij->tspij', mixing, table, precision=lax.Precision.HIGHEST).astype(jnp.bfloat16)
    vertical = jnp.einsum('tspij,jtk->tspik', mixed.astype(jnp.float32), windows.astype(jnp.float32),
                          precision=lax.Precision.HIGHEST).astype(jnp.bfloat16)
    across = jnp.swapaxes(table, 2, 3).astype(jnp.bfloat16)
    matched = jnp.einsum('tspik,spkl->til', vertical.astype(jnp.float32), across.astype(jnp.float32),
                         precision=lax.Precision.HIGHEST)
    science_tiles = science_strip.reshape(TILE, TILES_DEV, TILE).transpose(1, 0, 2)
    return science_tiles - matched


def reference(science, patches, margin, kernel_coef, ccd_first):
    templ16 = patches.astype(jnp.bfloat16)
    patch_ids = margin[:, 0]
    down = margin[:, 1]
    right = margin[:, 2]
    aligned = shift_tiles(jnp.take(templ16, patch_ids, axis=0), down, right)
    strips = aligned.reshape(OWNERS, TILES_DEV, TILE, TILE).transpose(0, 2, 1, 3).reshape(OWNERS, TILE, STRIP)
    device_ids = jnp.arange(OWNERS)
    keep_top = (device_ids > 0) & (ccd_first == 0)
    next_first = jnp.concatenate([ccd_first[1:], jnp.ones((1,), jnp.int32)])
    keep_bottom = next_first == 0
    zero_rows = jnp.zeros((1, RADIUS, STRIP), jnp.bfloat16)
    above = jnp.concatenate([zero_rows, strips[:-1, TILE - RADIUS:, :]], axis=0)
    below = jnp.concatenate([strips[1:, :RADIUS, :], zero_rows], axis=0)
    above = jnp.where(keep_top[:, None, None], above, jnp.zeros_like(above))
    below = jnp.where(keep_bottom[:, None, None], below, jnp.zeros_like(below))
    extended = jnp.concatenate([above, strips, below], axis=1)
    extended = jnp.pad(extended, ((0, 0), (0, 0), (RADIUS, RADIUS)))
    science_blocks = science.reshape(OWNERS, TILE, STRIP)
    coef_blocks = kernel_coef.reshape(NBASIS, OWNERS, TILES_DEV).transpose(1, 0, 2)
    diffs = lax.map(lambda items: match_strip(items[0], items[1], items[2]),
                    (extended, science_blocks, coef_blocks))
    diffs = diffs.reshape(TILES, TILE, TILE)
    back = shift_tiles(diffs, -down, -right)
    sums = jax.ops.segment_sum(back, patch_ids, num_segments=PATCHES)
    counts = jax.ops.segment_sum(jnp.ones((TILES,), jnp.float32), patch_ids, num_segments=PATCHES)
    return sums / jnp.maximum(counts, 1.0)[:, None, None]
```

```python
import functools
import math

import jax
import jax.numpy as jnp
from jax import lax
from jax.experimental import pallas as pl
from jax.experimental.pallas import tpu as pltpu
from jax.sharding import PartitionSpec as P

RADIUS = 10
SIGMAS = 3
ORDERS = 3
PAIRS = SIGMAS * ORDERS
EDGE = 16
SIDE = 128
BF = jnp.bfloat16
F32 = jnp.float32


def sigma_of(g):
    return 0.75 * 2.0**g


def norm_of(g):
    sigma = sigma_of(g)
    return sum(math.exp(-u * u / (2.0 * sigma * sigma)) for u in range(-RADIUS, RADIUS + 1))


def basis_functions(u, g):
    sigma = sigma_of(g)
    inside = jnp.abs(u) <= RADIUS
    base = jnp.where(inside, jnp.exp(u * u * (-1.0 / (2.0 * sigma * sigma))) * (1.0 / norm_of(g)), 0.0)
    scaled = u * (1.0 / sigma)
    first = base * scaled
    return base, first, first * scaled


def named_tiles(margin, strip, owner, owners, per, owned, slots):
    valid = (strip >= 0) & (strip < owners)
    row = jnp.clip(strip, 0, owners - 1) * per
    tiles = [jnp.int32(0)] * slots
    locals_ = [jnp.int32(0)] * slots
    there = [jnp.int32(0)] * slots
    count = jnp.int32(0)
    for t in range(per):
        patch = margin[row + t, 0]
        who = lax.div(patch, jnp.int32(owned))
        named = ((who == owner) & valid).astype(jnp.int32)
        for k in range(slots):
            hit = (named == 1) & (count == k)
            tiles[k] = jnp.where(hit, jnp.int32(t), tiles[k])
            locals_[k] = jnp.where(hit, patch - who * owned, locals_[k])
            there[k] = jnp.where(hit, jnp.int32(1), there[k])
        count = count + named
    return tiles, locals_, there


def one_hot(size, shift):
    rows = lax.broadcasted_iota(jnp.int32, (size, size), 0)
    cols = lax.broadcasted_iota(jnp.int32, (size, size), 1)
    return jnp.where(((rows - cols + shift) & (size - 1)) == 0, 1.0, 0.0).astype(BF)


def moved(x, down, right):
    size = x.shape[0]
    a = jnp.dot(one_hot(size, -down), x, preferred_element_type=F32).astype(BF)
    return jnp.dot(a, one_hot(size, right), preferred_element_type=F32).astype(BF)


def match_kernel(
    owners, per, owned, tile, slots,
    margin, coef, ccd, patches_h, science_h,
    out_h,
    patches, science, stage, pool, ext, halo, tab, mixed, mixed_small, across, v_mid, v_out, diff, back,
    load_sem, tile_send, tile_recv, halo_send, halo_recv, back_send, back_recv, own_sem,
):
    d = lax.axis_index("visit")
    has_low, has_high = d > 0, d < owners - 1
    low, high = d - 1, d + 1
    half, quarter = tile // 2, tile // 4
    mid_depth, small_depth = half + 2 * EDGE, quarter + 2 * EDGE
    width = tile + 2 * SIDE
    strip = per * tile

    patch_load = pltpu.make_async_copy(patches_h, patches, load_sem.at[0])
    science_load = pltpu.make_async_copy(science_h, science, load_sem.at[1])
    patch_load.start()
    science_load.start()

    barrier = pltpu.get_barrier_semaphore()

    @pl.when(has_low)
    def _():
        pl.semaphore_signal(barrier, inc=1, device_id={"visit": low}, device_id_type=pl.DeviceIdType.MESH)

    @pl.when(has_high)
    def _():
        pl.semaphore_signal(barrier, inc=1, device_id={"visit": high}, device_id_type=pl.DeviceIdType.MESH)

    ext[:, pl.ds(0, SIDE)] = jnp.zeros((tile + 2 * EDGE, SIDE), BF)
    ext[:, pl.ds(SIDE + strip, SIDE)] = jnp.zeros((tile + 2 * EDGE, SIDE), BF)
    _, high_local, _ = named_tiles(margin, high, d, owners, per, owned, slots)
    _, low_local, _ = named_tiles(margin, low, d, owners, per, owned, slots)
    _, own_local, _ = named_tiles(margin, d, d, owners, per, owned, slots)
    patch_load.wait()

    def remote(src, dst, send, recv, target):
        return pltpu.make_async_remote_copy(
            src_ref=src, dst_ref=dst, send_sem=send, recv_sem=recv,
            device_id={"visit": target}, device_id_type=pl.DeviceIdType.MESH,
        )

    def tile_to_high(k, target):
        return remote(stage.at[k], pool.at[k], tile_send.at[k], tile_recv.at[k], target)

    def tile_to_low(k, target):
        j = slots + k
        return remote(stage.at[j], pool.at[2 * slots + k], tile_send.at[j], tile_recv.at[j], target)

    for k in range(slots):
        stage[k] = patches[high_local[k]].astype(BF)
        stage[slots + k] = patches[low_local[k]].astype(BF)
    pl.semaphore_wait(barrier, has_low.astype(jnp.int32) + has_high.astype(jnp.int32))
    for k in range(slots):

        @pl.when(has_high)
        def _():
            tile_to_high(k, high).start()

        @pl.when(has_low)
        def _():
            tile_to_low(k, low).start()

    for k in range(slots):
        pool[slots + k] = patches[own_local[k]].astype(BF)

    rows = lax.broadcasted_iota(jnp.int32, (half, mid_depth), 0)
    cols = lax.broadcasted_iota(jnp.int32, (half, mid_depth), 1)
    u = (cols - rows - EDGE).astype(F32)
    for g in range(SIGMAS):
        for v, table in enumerate(basis_functions(u, g)):
            tab[g * ORDERS + v] = table

    def mix_tile(t, carry):
        for g in range(SIGMAS):
            for h in range(ORDERS):
                p = g * ORDERS + h
                total = coef[p * ORDERS, t] * tab[g * ORDERS]
                for v in range(1, ORDERS):
                    total = total + coef[p * ORDERS + v, t] * tab[g * ORDERS + v]
                total = total.astype(BF)
                mixed[t, pl.ds(p * half, half), :] = total
                mixed_small[t, pl.ds(p * quarter, quarter), :] = total[:quarter, :small_depth]
        return carry

    lax.fori_loop(0, per, mix_tile, 0)

    def across_rows(b, carry):
        r = lax.broadcasted_iota(jnp.int32, (SIDE, tile), 0) + b * SIDE
        c = lax.broadcasted_iota(jnp.int32, (SIDE, tile), 1)
        w = (r - c - SIDE).astype(F32)
        for g in range(SIGMAS):
            for h, table in enumerate(basis_functions(w, g)):
                start = pl.multiple_of((g * ORDERS + h) * width + b * SIDE, SIDE)
                across[pl.ds(start, SIDE), :] = table.astype(BF)
        return carry

    lax.fori_loop(0, width // SIDE, across_rows, 0)

    who = [lax.div(margin[d * per + t, 0], jnp.int32(owned)) for t in range(per)]
    places = []
    for t in range(per):
        rank = jnp.int32(0)
        for s in range(t):
            rank = rank + (who[s] == who[t]).astype(jnp.int32)
        places.append(jnp.clip((who[t] - d + 1) * slots + rank, 0, 3 * slots - 1))

    @pl.when(has_low)
    def _():
        for k in range(slots):
            tile_to_high(k, low).wait_recv()

    @pl.when(has_high)
    def _():
        for k in range(slots):
            tile_to_low(k, high).wait_recv()

    def align(t, carry):
        place = places[0]
        for s in range(1, per):
            place = jnp.where(t == s, places[s], place)
        shifted = moved(pool[place], margin[d * per + t, 1], margin[d * per + t, 2])
        ext[pl.ds(EDGE, tile), pl.ds(pl.multiple_of(SIDE + t * tile, SIDE), tile)] = shifted
        return carry

    lax.fori_loop(0, per, align, 0)

    def halo_to_high(target):
        return remote(
            ext.at[pl.ds(tile, EDGE), pl.ds(SIDE, strip)], halo.at[0], halo_send.at[0], halo_recv.at[0], target
        )

    def halo_to_low(target):
        return remote(
            ext.at[pl.ds(EDGE, EDGE), pl.ds(SIDE, strip)], halo.at[1], halo_send.at[1], halo_recv.at[1], target
        )

    @pl.when(has_high)
    def _():
        halo_to_high(high).start()

    @pl.when(has_low)
    def _():
        halo_to_low(low).start()

    def window(first, depth, t):
        return ext[pl.ds(first, depth), pl.ds(pl.multiple_of(t * tile, SIDE), width)]

    def vertical_mid(t, carry):
        result = jnp.dot(mixed[t], window(quarter, mid_depth, t), preferred_element_type=F32).astype(BF)
        for p in range(PAIRS):
            v_mid[pl.ds(pl.multiple_of(t * half, half), half), pl.ds(p * width, width)] = result[p * half : (p + 1) * half]
        return carry

    lax.fori_loop(0, per, vertical_mid, 0)
    science_load.wait()

    def across_mid(t, carry):
        start = pl.multiple_of(t * half, half)
        matched = jnp.dot(v_mid[pl.ds(start, 2 * half), :], across[...], preferred_element_type=F32)
        for i in range(2):
            sky = science[pl.ds(quarter, half), pl.ds(pl.multiple_of((t + i) * tile, SIDE), tile)]
            diff[t + i, pl.ds(quarter, half), :] = (sky - matched[i * half : (i + 1) * half]).astype(BF)
        return carry

    lax.fori_loop(0, per // 2, lambda i, c: across_mid(2 * i, c), 0)

    @pl.when(has_low)
    def _():
        halo_to_high(low).wait_recv()

    @pl.when(has_high)
    def _():
        halo_to_low(high).wait_recv()

    keep_top = has_low & (ccd[d] == 0)
    keep_bottom = has_high & (ccd[jnp.minimum(d + 1, owners - 1)] == 0)
    nothing = jnp.zeros((EDGE, strip), BF)
    ext[pl.ds(0, EDGE), pl.ds(SIDE, strip)] = jnp.where(keep_top, halo[0], nothing)
    ext[pl.ds(EDGE + tile, EDGE), pl.ds(SIDE, strip)] = jnp.where(keep_bottom, halo[1], nothing)

    def vertical_out(t, carry):
        for i, first in enumerate((0, tile - quarter)):
            result = jnp.dot(mixed_small[t], window(first, small_depth, t), preferred_element_type=F32).astype(BF)
            start = pl.multiple_of(t * half + i * quarter, quarter)
            for p in range(PAIRS):
                v_out[pl.ds(start, quarter), pl.ds(p * width, width)] = result[p * quarter : (p + 1) * quarter]
        return carry

    lax.fori_loop(0, per, vertical_out, 0)

    def across_out(t, carry):
        start = pl.multiple_of(t * half, half)
        matched = jnp.dot(v_out[pl.ds(start, 2 * half), :], across[...], preferred_element_type=F32)
        for i in range(4):
            first = (i % 2) * (tile - quarter)
            s = t + i // 2
            sky = science[pl.ds(first, quarter), pl.ds(pl.multiple_of(s * tile, SIDE), tile)]
            diff[s, pl.ds(first, quarter), :] = (sky - matched[i * quarter : (i + 1) * quarter]).astype(BF)
        return carry

    lax.fori_loop(0, per // 2, lambda i, c: across_out(2 * i, c), 0)

    to_low, _, _ = named_tiles(margin, d, low, owners, per, owned, slots)
    to_high, _, _ = named_tiles(margin, d, high, owners, per, owned, slots)
    to_own, _, _ = named_tiles(margin, d, d, owners, per, owned, slots)

    def returned(t):
        return moved(diff[t], -margin[d * per + t, 1], -margin[d * per + t, 2])

    def back_to_low(k, target):
        return remote(back.at[k], out_h.at[2 * slots + k], back_send.at[k], back_recv.at[k], target)

    def back_to_high(k, target):
        j = 2 * slots + k
        return remote(back.at[j], out_h.at[k], back_send.at[slots + k], back_recv.at[slots + k], target)

    def own_copy(k):
        return pltpu.make_async_copy(back.at[slots + k], out_h.at[slots + k], own_sem.at[k])

    for k in range(slots):
        back[k] = returned(to_low[k])

        @pl.when(has_low)
        def _():
            back_to_low(k, low).start()

        back[2 * slots + k] = returned(to_high[k])

        @pl.when(has_high)
        def _():
            back_to_high(k, high).start()

    for k in range(slots):
        back[slots + k] = returned(to_own[k])
        own_copy(k).start()
    for k in range(slots):
        own_copy(k).wait()

    @pl.when(has_low)
    def _():
        for k in range(slots):
            tile_to_low(k, low).wait_send()
            back_to_low(k, low).wait_send()
        halo_to_low(low).wait_send()
        for k in range(slots):
            back_to_high(k, low).wait_recv()

    @pl.when(has_high)
    def _():
        for k in range(slots):
            tile_to_high(k, high).wait_send()
            back_to_high(k, high).wait_send()
        halo_to_high(high).wait_send()
        for k in range(slots):
            back_to_low(k, high).wait_recv()


def mean_kernel(owners, per, owned, slots, margin, arrived, out_h, sums, sems):
    d = lax.axis_index("visit")
    ids, there = [], []
    for strip in (d - 1, d, d + 1):
        _, local, present = named_tiles(margin, strip, d, owners, per, owned, slots)
        ids += local
        there += present

    def copy(p):
        return pltpu.make_async_copy(sums.at[p], out_h.at[p], sems.at[p])

    def patch(p, carry):
        hits = [((ids[j] == p) & (there[j] == 1)) for j in range(3 * slots)]
        count = sum(hit.astype(jnp.int32) for hit in hits)
        scale = 1.0 / jnp.maximum(jnp.full((1, 1), count, jnp.int32).astype(F32), 1.0)
        sums[p] = jnp.zeros(sums.shape[1:], F32)
        for j, hit in enumerate(hits):

            @pl.when(hit)
            def _():
                sums[p] += arrived[j].astype(F32) * scale

        copy(p).start()
        return carry

    lax.fori_loop(0, owned, patch, 0)

    def finish(p, carry):
        copy(p).wait()
        return carry

    lax.fori_loop(0, owned, finish, 0)


def body(science, patches, margin, kernel_coef, ccd_first):
    owners = lax.axis_size("visit")
    owned, tile = patches.shape[0], patches.shape[1]
    per = science.shape[1] // tile
    slots = per // 2
    half, quarter = tile // 2, tile // 4
    width = tile + 2 * SIDE
    strip = per * tile
    smem = pl.BlockSpec(memory_space=pltpu.SMEM)
    anywhere = pl.BlockSpec(memory_space=pl.ANY)
    dma = pltpu.SemaphoreType.DMA
    arrived = pl.pallas_call(
        functools.partial(match_kernel, owners, per, owned, tile, slots),
        out_shape=jax.ShapeDtypeStruct((3 * slots, tile, tile), BF),
        in_specs=[smem, smem, smem, anywhere, anywhere],
        out_specs=anywhere,
        scratch_shapes=[
            pltpu.VMEM((owned, tile, tile), F32),
            pltpu.VMEM((tile, strip), F32),
            pltpu.VMEM((2 * slots, tile, tile), BF),
            pltpu.VMEM((3 * slots, tile, tile), BF),
            pltpu.VMEM((tile + 2 * EDGE, strip + 2 * SIDE), BF),
            pltpu.VMEM((2, EDGE, strip), BF),
            pltpu.VMEM((PAIRS, half, half + 2 * EDGE), F32),
            pltpu.VMEM((per, PAIRS * half, half + 2 * EDGE), BF),
            pltpu.VMEM((per, PAIRS * quarter, quarter + 2 * EDGE), BF),
            pltpu.VMEM((PAIRS * width, tile), BF),
            pltpu.VMEM((per * half, PAIRS * width), BF),
            pltpu.VMEM((per * half, PAIRS * width), BF),
            pltpu.VMEM((per, tile, tile), BF),
            pltpu.VMEM((3 * slots, tile, tile), BF),
            dma((2,)),
            dma((2 * slots,)),
            dma((2 * slots,)),
            dma((2,)),
            dma((2,)),
            dma((2 * slots,)),
            dma((2 * slots,)),
            dma((slots,)),
        ],
        compiler_params=pltpu.CompilerParams(
            collective_id=0, has_side_effects=True, vmem_limit_bytes=48 * 1024 * 1024
        ),
        name="match",
    )(margin, kernel_coef, ccd_first, patches, science)
    return pl.pallas_call(
        functools.partial(mean_kernel, owners, per, owned, slots),
        out_shape=jax.ShapeDtypeStruct(patches.shape, F32),
        in_specs=[smem, pl.BlockSpec(memory_space=pltpu.VMEM)],
        out_specs=anywhere,
        scratch_shapes=[pltpu.VMEM(patches.shape, F32), dma((owned,))],
        compiler_params=pltpu.CompilerParams(vmem_limit_bytes=16 * 1024 * 1024),
        name="mean",
    )(margin, arrived)


def solution(mesh):
    in_specs = (
        P(("grp", "visit"), None),
        P(("grp", "visit"), None, None),
        P("grp", None),
        P(None, ("grp", "visit")),
        P("grp"),
    )
    out_specs = P(("grp", "visit"), None, None)
    return jax.shard_map(body, mesh=mesh, in_specs=in_specs, out_specs=out_specs, check_vma=False)
```

```python
import functools
import math

import jax
import jax.numpy as jnp
from jax import lax
from jax.experimental import pallas as pl
from jax.experimental.pallas import tpu as pltpu
from jax.sharding import PartitionSpec as P

RADIUS = 10
SIGMAS = 3
ORDERS = 3
PAIRS = SIGMAS * ORDERS
EDGE = 16
SIDE = 128
BF = jnp.bfloat16
F32 = jnp.float32


def sigma_of(g):
    return 0.75 * 2.0**g


def norm_of(g):
    sigma = sigma_of(g)
    return sum(math.exp(-u * u / (2.0 * sigma * sigma)) for u in range(-RADIUS, RADIUS + 1))


def basis_functions(u, g):
    sigma = sigma_of(g)
    inside = jnp.abs(u) <= RADIUS
    base = jnp.where(inside, jnp.exp(u * u * (-1.0 / (2.0 * sigma * sigma))) * (1.0 / norm_of(g)), 0.0)
    scaled = u * (1.0 / sigma)
    first = base * scaled
    return base, first, first * scaled


def named_tiles(margin, strip, owner, owners, per, owned, slots):
    valid = (strip >= 0) & (strip < owners)
    row = (jnp.clip(strip, 0, owners - 1) * per).astype(jnp.int32)
    tiles = [row] * slots
    locals_ = [jnp.int32(0)] * slots
    there = [jnp.int32(0)] * slots
    count = jnp.int32(0)
    for t in range(per):
        patch = margin[0, row + t]
        who = lax.div(patch, jnp.int32(owned))
        named = ((who == owner) & valid).astype(jnp.int32)
        for k in range(slots):
            hit = (named == 1) & (count == k)
            tiles[k] = jnp.where(hit, row + t, tiles[k])
            locals_[k] = jnp.where(hit, patch - who * owned, locals_[k])
            there[k] = jnp.where(hit, jnp.int32(1), there[k])
        count = count + named
    return tiles, locals_, there


def one_hot(size, shift):
    rows = lax.broadcasted_iota(jnp.int32, (size, size), 0)
    cols = lax.broadcasted_iota(jnp.int32, (size, size), 1)
    return jnp.where(((rows - cols + shift) & (size - 1)) == 0, 1.0, 0.0).astype(BF)


def moved(down, x, right):
    a = jnp.dot(down, x, preferred_element_type=F32).astype(BF)
    return jnp.dot(a, right, preferred_element_type=F32).astype(BF)


def match_kernel(
    owners, per, owned, tile, slots,
    margin, coef, ccd, patches_h, science_h,
    out_h,
    patches, science, stage, pool, forth, ext, halo, tab, mixed, across, column, diff, parcel, landed, back,
    load_sem, tile_send, tile_recv, halo_send, halo_recv, back_send, back_recv, out_sem,
):
    d = lax.axis_index("visit")
    has_low, has_high = d > 0, d < owners - 1
    low, high = d - 1, d + 1
    chunks = 4
    chunk = tile // chunks
    depth = chunk + 2 * EDGE
    width = tile + SIDE
    places = 3 * slots

    barrier = pltpu.get_barrier_semaphore()

    @pl.when(has_low)
    def _():
        pl.semaphore_signal(barrier, inc=1, device_id={"visit": low}, device_id_type=pl.DeviceIdType.MESH)

    @pl.when(has_high)
    def _():
        pl.semaphore_signal(barrier, inc=1, device_id={"visit": high}, device_id_type=pl.DeviceIdType.MESH)

    patch_load = pltpu.make_async_copy(patches_h, patches, load_sem.at[0])
    science_load = pltpu.make_async_copy(science_h, science, load_sem.at[1])
    patch_load.start()
    science_load.start()

    high_tiles, high_local, _ = named_tiles(margin, high, d, owners, per, owned, slots)
    low_tiles, low_local, _ = named_tiles(margin, low, d, owners, per, owned, slots)
    own_tiles, own_local, _ = named_tiles(margin, d, d, owners, per, owned, slots)
    from_low, _, _ = named_tiles(margin, d, low, owners, per, owned, slots)
    from_high, _, _ = named_tiles(margin, d, high, owners, per, owned, slots)
    arriving = from_low + own_tiles + from_high
    returning = low_tiles + own_tiles + high_tiles

    def remote(src, dst, send, recv, target):
        return pltpu.make_async_remote_copy(
            src_ref=src, dst_ref=dst, send_sem=send, recv_sem=recv,
            device_id={"visit": target}, device_id_type=pl.DeviceIdType.MESH,
        )

    def tile_to_high(k, target):
        return remote(stage.at[k], pool.at[k], tile_send.at[k], tile_recv.at[k], target)

    def tile_to_low(k, target):
        j = slots + k
        return remote(stage.at[j], pool.at[2 * slots + k], tile_send.at[j], tile_recv.at[j], target)

    patch_load.wait()
    for k in range(slots):
        stage[k] = patches[high_local[k]].astype(BF)
        stage[slots + k] = patches[low_local[k]].astype(BF)
    pl.semaphore_wait(barrier, has_low.astype(jnp.int32) + has_high.astype(jnp.int32))
    for k in range(slots):

        @pl.when(has_high)
        def _():
            tile_to_high(k, high).start()

        @pl.when(has_low)
        def _():
            tile_to_low(k, low).start()

    for k in range(slots):
        pool[slots + k] = patches[own_local[k]].astype(BF)

    def align(j):
        t = arriving[j]
        forth[j] = moved(one_hot(tile, -margin[1, t]), pool[j], one_hot(tile, margin[2, t]))

    rows = lax.broadcasted_iota(jnp.int32, (chunk, depth), 0)
    cols = lax.broadcasted_iota(jnp.int32, (chunk, depth), 1)
    u = (cols - rows - EDGE).astype(F32)
    for g in range(SIGMAS):
        for v, table in enumerate(basis_functions(u, g)):
            tab[g * ORDERS + v] = table

    def mix_tile(t, carry):
        for g in range(SIGMAS):
            for h in range(ORDERS):
                p = g * ORDERS + h
                total = coef[t, p * ORDERS] * tab[g * ORDERS]
                for v in range(1, ORDERS):
                    total = total + coef[t, p * ORDERS + v] * tab[g * ORDERS + v]
                mixed[t, pl.ds(p * chunk, chunk), :] = total.astype(BF)
        return carry

    lax.fori_loop(0, per, mix_tile, 0)

    def across_rows(b, carry):
        r = lax.broadcasted_iota(jnp.int32, (SIDE, tile), 0)
        c = lax.broadcasted_iota(jnp.int32, (SIDE, tile), 1)
        side = jnp.where(r < SIDE // 2, r + tile, r - SIDE)
        w = (jnp.where(b * SIDE < tile, r + b * SIDE, side) - c).astype(F32)
        for g in range(SIGMAS):
            for h, table in enumerate(basis_functions(w, g)):
                start = pl.multiple_of((g * ORDERS + h) * width + b * SIDE, SIDE)
                across[pl.ds(start, SIDE), :] = table.astype(BF)
        return carry

    lax.fori_loop(0, width // SIDE, across_rows, 0)

    for k in range(slots):
        align(slots + k)

    who = [lax.div(margin[0, d * per + t], jnp.int32(owned)) for t in range(per)]
    place = []
    for t in range(per):
        rank = jnp.int32(0)
        for s in range(t):
            rank = rank + (who[s] == who[t]).astype(jnp.int32)
        place.append(jnp.clip((who[t] - d + 1) * slots + rank, 0, places - 1))

    for k in range(slots):

        @pl.when(has_low)
        def _():
            tile_to_high(k, low).wait_recv()
            align(k)

        @pl.when(has_high)
        def _():
            tile_to_low(k, high).wait_recv()
            align(2 * slots + k)

    for t in range(per):
        ext[t, pl.ds(EDGE, tile), pl.ds(0, tile)] = forth[place[t]]

    def halo_to_high(target):
        return remote(
            ext.at[:, pl.ds(tile, EDGE), pl.ds(0, tile)], halo.at[0], halo_send.at[0], halo_recv.at[0], target
        )

    def halo_to_low(target):
        return remote(
            ext.at[:, pl.ds(EDGE, EDGE), pl.ds(0, tile)], halo.at[1], halo_send.at[1], halo_recv.at[1], target
        )

    @pl.when(has_high)
    def _():
        halo_to_high(high).start()

    @pl.when(has_low)
    def _():
        halo_to_low(low).start()

    def fill_sides(first, count):
        lane = lax.broadcasted_iota(jnp.int32, (count, SIDE), 1)
        none = jnp.zeros((count, SIDE), F32)
        for t in range(per):
            right = ext[t + 1, pl.ds(first, count), pl.ds(0, SIDE)].astype(F32) if t + 1 < per else none
            left = ext[t - 1, pl.ds(first, count), pl.ds(tile - SIDE, SIDE)].astype(F32) if t > 0 else none
            ext[t, pl.ds(first, count), pl.ds(tile, SIDE)] = jnp.where(lane < SIDE // 2, right, left).astype(BF)

    fill_sides(EDGE, tile)
    science_load.wait()

    def chunk_to_low(k, c, target):
        at = pl.ds(pl.multiple_of(c * chunk, chunk), chunk)
        return remote(
            parcel.at[k, at], landed.at[slots + k, at], back_send.at[c, k], back_recv.at[c, k], target
        )

    def chunk_to_high(k, c, target):
        j = slots + k
        at = pl.ds(pl.multiple_of(c * chunk, chunk), chunk)
        return remote(parcel.at[j, at], landed.at[k, at], back_send.at[c, j], back_recv.at[c, j], target)

    def one_chunk(i, carry):
        c = lax.rem(i + 1, chunks)
        at = pl.ds(pl.multiple_of(c * chunk, chunk), chunk)

        @pl.when(i == chunks - 2)
        def _():
            @pl.when(has_low)
            def _():
                halo_to_high(low).wait_recv()

            @pl.when(has_high)
            def _():
                halo_to_low(high).wait_recv()

            keep_top = has_low & (ccd[d] == 0)
            keep_bottom = has_high & (ccd[jnp.minimum(d + 1, owners - 1)] == 0)
            nothing = jnp.zeros((EDGE, tile), BF)
            for t in range(per):
                ext[t, pl.ds(0, EDGE), pl.ds(0, tile)] = jnp.where(keep_top, halo[0, t], nothing)
                ext[t, pl.ds(EDGE + tile, EDGE), pl.ds(0, tile)] = jnp.where(keep_bottom, halo[1, t], nothing)
            fill_sides(0, EDGE)
            fill_sides(EDGE + tile, EDGE)

        window = pl.ds(pl.multiple_of(c * chunk, chunk), depth)
        for t in range(per):
            result = jnp.dot(mixed[t], ext[t, window, :], preferred_element_type=F32).astype(BF)
            for p in range(PAIRS):
                column[pl.ds(t * chunk, chunk), pl.ds(p * width, width)] = result[p * chunk : (p + 1) * chunk]
        matched = jnp.dot(column[...], across[...], preferred_element_type=F32)
        for t in range(per):
            sky = science[at, pl.ds(t * tile, tile)]
            diff[t, at, :] = (sky - matched[t * chunk : (t + 1) * chunk]).astype(BF)
        for k in range(slots):
            parcel[k, at, :] = diff[from_low[k] - d * per, at, :]
            parcel[slots + k, at, :] = diff[from_high[k] - d * per, at, :]

            @pl.when(has_low)
            def _():
                chunk_to_low(k, c, low).start()

            @pl.when(has_high)
            def _():
                chunk_to_high(k, c, high).start()

        return carry

    lax.fori_loop(0, chunks, one_chunk, 0)

    def out_copy(j):
        return pltpu.make_async_copy(back.at[j], out_h.at[j], out_sem.at[j])

    def unshift(j, x):
        t = returning[j]
        back[j] = moved(one_hot(tile, margin[1, t]), x, one_hot(tile, -margin[2, t]))
        out_copy(j).start()

    for k in range(slots):
        unshift(slots + k, diff[own_tiles[k] - d * per])
    for k in range(slots):

        @pl.when(has_low)
        def _():
            for c in range(chunks):
                chunk_to_high(k, c, low).wait_recv()
            unshift(k, landed[k])

        @pl.when(has_high)
        def _():
            for c in range(chunks):
                chunk_to_low(k, c, high).wait_recv()
            unshift(2 * slots + k, landed[slots + k])

    for k in range(slots):
        out_copy(slots + k).wait()

    @pl.when(has_low)
    def _():
        for k in range(slots):
            tile_to_low(k, low).wait_send()
            for c in range(chunks):
                chunk_to_low(k, c, low).wait_send()
        halo_to_low(low).wait_send()
        for k in range(slots):
            out_copy(k).wait()

    @pl.when(has_high)
    def _():
        for k in range(slots):
            tile_to_high(k, high).wait_send()
            for c in range(chunks):
                chunk_to_high(k, c, high).wait_send()
        halo_to_high(high).wait_send()
        for k in range(slots):
            out_copy(2 * slots + k).wait()


def mean_kernel(owners, per, owned, slots, margin, arrived_h, out_h, arrived, nothing, sums, load_sem, sems):
    d = lax.axis_index("visit")
    load = pltpu.make_async_copy(arrived_h, arrived, load_sem)
    load.start()
    nothing[...] = jnp.zeros(nothing.shape, F32)
    ids, there = [], []
    for strip in (d - 1, d, d + 1):
        _, local, present = named_tiles(margin, strip, d, owners, per, owned, slots)
        ids += local
        there += present

    def hits_of(p):
        hits = [((ids[j] == p) & (there[j] == 1)) for j in range(3 * slots)]
        return hits, sum(hit.astype(jnp.int32) for hit in hits)

    def zero(p, carry):
        @pl.when(hits_of(p)[1] == 0)
        def _():
            pltpu.make_async_copy(nothing, out_h.at[p], sems.at[p]).start()

        return carry

    lax.fori_loop(0, owned, zero, 0)
    load.wait()

    def patch(p, carry):
        hits, count = hits_of(p)
        scale = 1.0 / jnp.maximum(jnp.full((1, 1), count, jnp.int32).astype(F32), 1.0)
        before = jnp.int32(0)
        for j, hit in enumerate(hits):

            @pl.when(hit & (before == 0))
            def _():
                sums[p] = arrived[j].astype(F32) * scale

            @pl.when(hit & (before > 0))
            def _():
                sums[p] += arrived[j].astype(F32) * scale

            before = before + hit.astype(jnp.int32)

        @pl.when(count > 0)
        def _():
            pltpu.make_async_copy(sums.at[p], out_h.at[p], sems.at[p]).start()

        return carry

    lax.fori_loop(0, owned, patch, 0)

    def finish(p, carry):
        pltpu.make_async_copy(sums.at[p], out_h.at[p], sems.at[p]).wait()
        return carry

    lax.fori_loop(0, owned, finish, 0)


def body(science, patches, margin, kernel_coef, ccd_first):
    owners = lax.axis_size("visit")
    owned, tile = patches.shape[0], patches.shape[1]
    per = science.shape[1] // tile
    slots = per // 2
    chunks = 4
    chunk = tile // chunks
    depth = chunk + 2 * EDGE
    width = tile + SIDE
    smem = pl.BlockSpec(memory_space=pltpu.SMEM)
    anywhere = pl.BlockSpec(memory_space=pl.ANY)
    dma = pltpu.SemaphoreType.DMA
    margin = margin.T
    arrived = pl.pallas_call(
        functools.partial(match_kernel, owners, per, owned, tile, slots),
        out_shape=jax.ShapeDtypeStruct((3 * slots, tile, tile), BF),
        in_specs=[smem, smem, smem, anywhere, anywhere],
        out_specs=anywhere,
        scratch_shapes=[
            pltpu.VMEM((owned, tile, tile), F32),
            pltpu.VMEM((tile, per * tile), F32),
            pltpu.VMEM((2 * slots, tile, tile), BF),
            pltpu.VMEM((3 * slots, tile, tile), BF),
            pltpu.VMEM((3 * slots, tile, tile), BF),
            pltpu.VMEM((per, tile + 2 * EDGE, width), BF),
            pltpu.VMEM((2, per, EDGE, tile), BF),
            pltpu.VMEM((PAIRS, chunk, depth), F32),
            pltpu.VMEM((per, PAIRS * chunk, depth), BF),
            pltpu.VMEM((PAIRS * width, tile), BF),
            pltpu.VMEM((per * chunk, PAIRS * width), BF),
            pltpu.VMEM((per, tile, tile), BF),
            pltpu.VMEM((2 * slots, tile, tile), BF),
            pltpu.VMEM((2 * slots, tile, tile), BF),
            pltpu.VMEM((3 * slots, tile, tile), BF),
            dma((2,)),
            dma((2 * slots,)),
            dma((2 * slots,)),
            dma((2,)),
            dma((2,)),
            dma((chunks, 2 * slots)),
            dma((chunks, 2 * slots)),
            dma((3 * slots,)),
        ],
        compiler_params=pltpu.CompilerParams(
            collective_id=0, has_side_effects=True, vmem_limit_bytes=64 * 1024 * 1024
        ),
        name="match",
    )(margin, kernel_coef.T, ccd_first, patches, science)
    return pl.pallas_call(
        functools.partial(mean_kernel, owners, per, owned, slots),
        out_shape=jax.ShapeDtypeStruct(patches.shape, F32),
        in_specs=[smem, anywhere],
        out_specs=anywhere,
        scratch_shapes=[
            pltpu.VMEM(arrived.shape, BF),
            pltpu.VMEM((tile, tile), F32),
            pltpu.VMEM(patches.shape, F32),
            dma(()),
            dma((owned,)),
        ],
        compiler_params=pltpu.CompilerParams(vmem_limit_bytes=64 * 1024 * 1024),
        name="mean",
    )(margin, arrived)


def solution(mesh):
    in_specs = (
        P(("grp", "visit"), None),
        P(("grp", "visit"), None, None),
        P("grp", None),
        P(None, ("grp", "visit")),
        P("grp"),
    )
    out_specs = P(("grp", "visit"), None, None)
    return jax.shard_map(body, mesh=mesh, in_specs=in_specs, out_specs=out_specs, check_vma=False)
```

```python
import functools
import math

import jax
import jax.numpy as jnp
from jax import lax
from jax.experimental import pallas as pl
from jax.experimental.pallas import tpu as pltpu
from jax.sharding import PartitionSpec as P

RADIUS = 10
SIGMAS = 3
ORDERS = 3
PAIRS = SIGMAS * ORDERS
EDGE = 16
SIDE = 128
BF = jnp.bfloat16
F32 = jnp.float32


def sigma_of(g):
    return 0.75 * 2.0**g


def norm_of(g):
    sigma = sigma_of(g)
    return sum(math.exp(-u * u / (2.0 * sigma * sigma)) for u in range(-RADIUS, RADIUS + 1))


def basis_functions(u, g):
    sigma = sigma_of(g)
    inside = jnp.abs(u) <= RADIUS
    base = jnp.where(inside, jnp.exp(u * u * (-1.0 / (2.0 * sigma * sigma))) * (1.0 / norm_of(g)), 0.0)
    scaled = u * (1.0 / sigma)
    first = base * scaled
    return base, first, first * scaled


def named_tiles(margin, strip, owner, owners, per, owned, slots):
    valid = (strip >= 0) & (strip < owners)
    row = (jnp.clip(strip, 0, owners - 1) * per).astype(jnp.int32)
    tiles = [row] * slots
    locals_ = [jnp.int32(0)] * slots
    there = [jnp.int32(0)] * slots
    count = jnp.int32(0)
    for t in range(per):
        patch = margin[0, row + t]
        who = lax.div(patch, jnp.int32(owned))
        named = ((who == owner) & valid).astype(jnp.int32)
        for k in range(slots):
            hit = (named == 1) & (count == k)
            tiles[k] = jnp.where(hit, row + t, tiles[k])
            locals_[k] = jnp.where(hit, patch - who * owned, locals_[k])
            there[k] = jnp.where(hit, jnp.int32(1), there[k])
        count = count + named
    return tiles, locals_, there


def one_hot(size, shift):
    rows = lax.broadcasted_iota(jnp.int32, (size, size), 0)
    cols = lax.broadcasted_iota(jnp.int32, (size, size), 1)
    return jnp.where(((rows - cols + shift) & (size - 1)) == 0, 1.0, 0.0).astype(BF)


def moved(down, x, right):
    a = jnp.dot(down, x, preferred_element_type=F32).astype(BF)
    return jnp.dot(a, right, preferred_element_type=F32).astype(BF)


def match_kernel(
    owners, per, owned, tile, slots,
    margin, ccd, coef, patches_h, science_h,
    out_h,
    patches, science, sky_out, sky, coefs, ext, frame, frames, halo_out, halo, reply, reply_out, replies,
    tab, mixed, across, across_side, column, side_rows, side_column, matched, back,
    load_sem, coef_send, coef_recv, frame_send, frame_recv, halo_send, halo_recv, reply_send, reply_recv,
    sky_send, sky_recv, out_sem,
):
    d = lax.axis_index("visit")
    has_low, has_high = d > 0, d < owners - 1
    low, high = d - 1, d + 1
    chunks = 4
    chunk = tile // chunks
    depth = chunk + 2 * EDGE
    places = 3 * slots

    barrier = pltpu.get_barrier_semaphore()

    @pl.when(has_low)
    def _():
        pl.semaphore_signal(barrier, inc=1, device_id={"visit": low}, device_id_type=pl.DeviceIdType.MESH)

    @pl.when(has_high)
    def _():
        pl.semaphore_signal(barrier, inc=1, device_id={"visit": high}, device_id_type=pl.DeviceIdType.MESH)

    patch_load = pltpu.make_async_copy(patches_h, patches, load_sem.at[0])
    patch_load.start()
    science_loads = [
        pltpu.make_async_copy(science_h.at[:, pl.ds(t * tile, tile)], science.at[t], load_sem.at[1 + t])
        for t in range(per)
    ]
    for load in science_loads:
        load.start()

    high_tiles, high_local, _ = named_tiles(margin, high, d, owners, per, owned, slots)
    low_tiles, low_local, _ = named_tiles(margin, low, d, owners, per, owned, slots)
    own_tiles, own_local, _ = named_tiles(margin, d, d, owners, per, owned, slots)
    from_low, _, _ = named_tiles(margin, d, low, owners, per, owned, slots)
    from_high, _, _ = named_tiles(margin, d, high, owners, per, owned, slots)
    held = low_tiles + own_tiles + high_tiles
    held_local = low_local + own_local + high_local
    first_slot = pl.ds(0, slots)
    last_slot = pl.ds(2 * slots, slots)

    def pair(src_high, dst_high, src_low, dst_low, send, recv, k):
        def to_high(target):
            return pltpu.make_async_remote_copy(
                src_ref=src_high, dst_ref=dst_high, send_sem=send.at[k], recv_sem=recv.at[k],
                device_id={"visit": target}, device_id_type=pl.DeviceIdType.MESH,
            )

        def to_low(target):
            return pltpu.make_async_remote_copy(
                src_ref=src_low, dst_ref=dst_low, send_sem=send.at[k + 1], recv_sem=recv.at[k + 1],
                device_id={"visit": target}, device_id_type=pl.DeviceIdType.MESH,
            )

        def start():
            @pl.when(has_high)
            def _():
                to_high(high).start()

            @pl.when(has_low)
            def _():
                to_low(low).start()

        def arrive():
            @pl.when(has_low)
            def _():
                to_high(low).wait_recv()

            @pl.when(has_high)
            def _():
                to_low(high).wait_recv()

        def sent():
            @pl.when(has_high)
            def _():
                to_high(high).wait_send()

            @pl.when(has_low)
            def _():
                to_low(low).wait_send()

        return start, arrive, sent

    coef_start, coef_arrive, coef_sent = pair(
        coefs.at[1], coefs.at[0], coefs.at[1], coefs.at[2], coef_send, coef_recv, 0
    )
    frame_start, frame_arrive, frame_sent = pair(
        frame.at[last_slot], frames.at[first_slot], frame.at[first_slot], frames.at[last_slot],
        frame_send, frame_recv, 0,
    )
    halo_start, halo_arrive, halo_sent = pair(
        halo_out.at[0], halo.at[0], halo_out.at[1], halo.at[1], halo_send, halo_recv, 0
    )
    reply_start, reply_arrive, reply_sent = pair(
        reply_out.at[1], replies.at[first_slot], reply_out.at[0], replies.at[last_slot], reply_send, reply_recv, 0
    )
    skies = [
        pair(
            sky_out.at[slots + k], sky.at[k], sky_out.at[k], sky.at[2 * slots + k], sky_send, sky_recv, 2 * k
        )
        for k in range(slots)
    ]

    coefs[1] = jnp.zeros(coefs.shape[1:], F32)
    coefs[1, pl.ds(0, coef.shape[0]), pl.ds(0, coef.shape[1])] = coef[...]
    patch_load.wait()
    pl.semaphore_wait(barrier, has_low.astype(jnp.int32) + has_high.astype(jnp.int32))
    coef_start()

    rows = lax.broadcasted_iota(jnp.int32, (2 * EDGE, tile), 0)
    cols = lax.broadcasted_iota(jnp.int32, (2 * EDGE, tile), 1)
    border = jnp.where(cols == jnp.where(rows < EDGE, rows, rows + tile - 2 * EDGE), 1.0, 0.0).astype(BF)
    for j in range(places):
        t = held[j]
        x = moved(one_hot(tile, -margin[1, t]), patches[held_local[j]].astype(BF), one_hot(tile, margin[2, t]))
        ext[j, pl.ds(EDGE, tile), pl.ds(0, tile)] = x
        frame[j, pl.ds(0, EDGE), :] = x[:EDGE]
        frame[j, pl.ds(EDGE, EDGE), :] = x[tile - EDGE :]
        frame[j, pl.ds(2 * EDGE, 2 * EDGE), :] = lax.dot_general(
            border, x, (((1,), (1,)), ((), ())), preferred_element_type=F32
        ).astype(BF)
    frame_start()
    for k in range(slots):
        frames[slots + k] = frame[slots + k]

    for load in science_loads:
        load.wait()
    for k in range(slots):
        sky_out[k] = science[from_low[k] - d * per].astype(BF)
        sky_out[slots + k] = science[from_high[k] - d * per].astype(BF)
        sky[slots + k] = science[own_tiles[k] - d * per].astype(BF)
    skies[0][0]()

    rows = lax.broadcasted_iota(jnp.int32, (chunk, depth), 0)
    cols = lax.broadcasted_iota(jnp.int32, (chunk, depth), 1)
    u = (cols - rows - EDGE).astype(F32)
    for g in range(SIGMAS):
        for v, table in enumerate(basis_functions(u, g)):
            tab[g * ORDERS + v] = table

    def across_rows(b, carry):
        r = lax.broadcasted_iota(jnp.int32, (SIDE, tile), 0)
        c = lax.broadcasted_iota(jnp.int32, (SIDE, tile), 1)
        side = jnp.where(r < SIDE // 2, r + tile, r - SIDE)
        main = b * SIDE < tile
        w = (jnp.where(main, r + b * SIDE, side) - c).astype(F32)
        for g in range(SIGMAS):
            for h, table in enumerate(basis_functions(w, g)):
                p = g * ORDERS + h
                table = table.astype(BF)

                @pl.when(main)
                def _():
                    across[pl.ds(pl.multiple_of(p * tile + b * SIDE, SIDE), SIDE), :] = table

                @pl.when(jnp.logical_not(main))
                def _():
                    across_side[pl.ds(p * SIDE, SIDE), :] = table

        return carry

    lax.fori_loop(0, tile // SIDE + 1, across_rows, 0)

    coef_arrive()
    for j in range(places):
        of = j // slots
        start = jnp.clip(d + of - 1, 0, owners - 1) * per
        weights = coefs[of, pl.ds(held[j] - start, 1), :]
        for g in range(SIGMAS):
            for h in range(ORDERS):
                p = g * ORDERS + h
                total = weights[:, p * ORDERS : p * ORDERS + 1] * tab[g * ORDERS]
                for v in range(1, ORDERS):
                    at = p * ORDERS + v
                    total = total + weights[:, at : at + 1] * tab[g * ORDERS + v]
                mixed[j, pl.ds(p * chunk, chunk), :] = total.astype(BF)

    who = [lax.div(margin[0, d * per + t], jnp.int32(owned)) for t in range(per)]
    place = []
    for t in range(per):
        rank = jnp.int32(0)
        for s in range(t):
            rank = rank + (who[s] == who[t]).astype(jnp.int32)
        place.append(jnp.clip((who[t] - d + 1) * slots + rank, 0, places - 1))

    frame_arrive()
    for t in range(per):
        f = frames[place[t]]
        halo_out[0, t] = f[EDGE : 2 * EDGE]
        halo_out[1, t] = f[:EDGE]
        reply[t, pl.ds(2 * EDGE, 2 * EDGE), pl.ds(tile, SIDE)] = jnp.zeros((2 * EDGE, SIDE), BF)
        if t + 1 < per:
            reply[t + 1, pl.ds(2 * EDGE, EDGE), pl.ds(0, tile)] = f[3 * EDGE :]
        if t > 0:
            reply[t - 1, pl.ds(3 * EDGE, EDGE), pl.ds(0, tile)] = f[2 * EDGE : 3 * EDGE]
    reply[0, pl.ds(2 * EDGE, EDGE), pl.ds(0, tile)] = jnp.zeros((EDGE, tile), BF)
    reply[per - 1, pl.ds(3 * EDGE, EDGE), pl.ds(0, tile)] = jnp.zeros((EDGE, tile), BF)
    halo_start()

    def hand_back():
        halo_arrive()
        keep = (
            has_low & (ccd[d] == 0),
            has_high & (ccd[jnp.minimum(d + 1, owners - 1)] == 0),
        )
        nothing = jnp.zeros((EDGE, tile), BF)
        lane = lax.broadcasted_iota(jnp.int32, (EDGE, SIDE), 1)
        none = jnp.zeros((EDGE, SIDE), F32)
        for i in range(2):
            parts = [jnp.where(keep[i], halo[i, t], nothing) for t in range(per)]
            for t in range(per):
                right = parts[t + 1][:, :SIDE].astype(F32) if t + 1 < per else none
                left = parts[t - 1][:, tile - SIDE :].astype(F32) if t > 0 else none
                at = pl.ds(i * EDGE, EDGE)
                reply[t, at, pl.ds(0, tile)] = parts[t]
                reply[t, at, pl.ds(tile, SIDE)] = jnp.where(lane < SIDE // 2, right, left).astype(BF)
        for k in range(slots):
            reply_out[0, k] = reply[from_low[k] - d * per]
            reply_out[1, k] = reply[from_high[k] - d * per]
            replies[slots + k] = reply[own_tiles[k] - d * per]
        reply_start()
        for k in range(1, slots):
            skies[k][0]()

    def surround():
        reply_arrive()
        r = lax.broadcasted_iota(jnp.int32, (2 * EDGE, SIDE), 0)
        c = lax.broadcasted_iota(jnp.int32, (2 * EDGE, SIDE), 1)
        spread = jnp.where(c == jnp.where(r < EDGE, r + SIDE - EDGE, r - EDGE), 1.0, 0.0).astype(BF)
        for j in range(places):
            ext[j, pl.ds(0, EDGE), :] = replies[j, pl.ds(0, EDGE), :]
            ext[j, pl.ds(EDGE + tile, EDGE), :] = replies[j, pl.ds(EDGE, EDGE), :]
            ext[j, pl.ds(EDGE, tile), pl.ds(tile, SIDE)] = lax.dot_general(
                replies[j, pl.ds(2 * EDGE, 2 * EDGE), pl.ds(0, tile)], spread,
                (((0,), (0,)), ((), ())), preferred_element_type=F32,
            ).astype(BF)

    def one_chunk(i, carry):
        c = lax.rem(i + 1, chunks)

        @pl.when(i == 1)
        def _():
            hand_back()

        @pl.when(i == chunks - 2)
        def _():
            surround()

        window = pl.ds(pl.multiple_of(c * chunk, chunk), depth)
        for j in range(places):
            result = jnp.dot(mixed[j], ext[j, window, pl.ds(0, tile)], preferred_element_type=F32).astype(BF)
            for p in range(PAIRS):
                column[pl.ds(j * chunk, chunk), pl.ds(p * tile, tile)] = result[p * chunk : (p + 1) * chunk]
        matched[c] = jnp.dot(column[...], across[...], preferred_element_type=F32)
        return carry

    lax.fori_loop(0, chunks, one_chunk, 0)

    for j in range(places):
        for c in range(chunks):
            side_rows[j, :, pl.ds(c * SIDE, SIDE)] = ext[j, pl.ds(c * chunk, depth), pl.ds(tile, SIDE)]

    def side_tile(j, carry):
        result = jnp.dot(mixed[j], side_rows[j], preferred_element_type=F32).astype(BF)
        for c in range(chunks):
            start = pl.multiple_of((j * chunks + c) * chunk, chunk)
            for p in range(PAIRS):
                side_column[pl.ds(start, chunk), pl.ds(p * SIDE, SIDE)] = result[
                    p * chunk : (p + 1) * chunk, c * SIDE : (c + 1) * SIDE
                ]
        return carry

    lax.fori_loop(0, places, side_tile, 0, unroll=2)
    for start, arrive, sent in skies:
        arrive()

    def out_copy(j):
        return pltpu.make_async_copy(back.at[j], out_h.at[j], out_sem.at[j])

    for j in range(places):
        sides = jnp.dot(
            side_column[pl.ds(j * tile, tile), :], across_side[...], preferred_element_type=F32
        )
        whole = jnp.concatenate([matched[c, pl.ds(j * chunk, chunk), :] for c in range(chunks)], axis=0)
        diff = (sky[j].astype(F32) - (whole + sides)).astype(BF)
        t = held[j]
        back[j] = moved(one_hot(tile, margin[1, t]), diff, one_hot(tile, -margin[2, t]))
        out_copy(j).start()

    for j in range(places):
        out_copy(j).wait()
    for sent in [coef_sent, frame_sent, halo_sent, reply_sent] + [sky_pair[2] for sky_pair in skies]:
        sent()


def mean_kernel(owners, per, owned, slots, margin, arrived_h, out_h, arrived, nothing, sums, load_sem, sems):
    d = lax.axis_index("visit")
    load = pltpu.make_async_copy(arrived_h, arrived, load_sem)
    load.start()
    nothing[...] = jnp.zeros(nothing.shape, F32)
    ids, there = [], []
    for strip in (d - 1, d, d + 1):
        _, local, present = named_tiles(margin, strip, d, owners, per, owned, slots)
        ids += local
        there += present

    def hits_of(p):
        hits = [((ids[j] == p) & (there[j] == 1)) for j in range(3 * slots)]
        return hits, sum(hit.astype(jnp.int32) for hit in hits)

    def zero(p, carry):
        @pl.when(hits_of(p)[1] == 0)
        def _():
            pltpu.make_async_copy(nothing, out_h.at[p], sems.at[p]).start()

        return carry

    lax.fori_loop(0, owned, zero, 0)
    load.wait()

    def patch(p, carry):
        hits, count = hits_of(p)
        scale = 1.0 / jnp.maximum(jnp.full((1, 1), count, jnp.int32).astype(F32), 1.0)
        before = jnp.int32(0)
        for j, hit in enumerate(hits):

            @pl.when(hit & (before == 0))
            def _():
                sums[p] = arrived[j].astype(F32) * scale

            @pl.when(hit & (before > 0))
            def _():
                sums[p] += arrived[j].astype(F32) * scale

            before = before + hit.astype(jnp.int32)

        @pl.when(count > 0)
        def _():
            pltpu.make_async_copy(sums.at[p], out_h.at[p], sems.at[p]).start()

        return carry

    lax.fori_loop(0, owned, patch, 0)

    def finish(p, carry):
        pltpu.make_async_copy(sums.at[p], out_h.at[p], sems.at[p]).wait()
        return carry

    lax.fori_loop(0, owned, finish, 0)


def body(science, patches, margin, kernel_coef, ccd_first):
    owners = lax.axis_size("visit")
    owned, tile = patches.shape[0], patches.shape[1]
    per = science.shape[1] // tile
    slots = per // 2
    chunks = 4
    chunk = tile // chunks
    depth = chunk + 2 * EDGE
    width = tile + SIDE
    smem = pl.BlockSpec(memory_space=pltpu.SMEM)
    anywhere = pl.BlockSpec(memory_space=pl.ANY)
    dma = pltpu.SemaphoreType.DMA
    margin = margin.T
    places = 3 * slots
    arrived = pl.pallas_call(
        functools.partial(match_kernel, owners, per, owned, tile, slots),
        out_shape=jax.ShapeDtypeStruct((places, tile, tile), BF),
        in_specs=[smem, smem, pl.BlockSpec(memory_space=pltpu.VMEM), anywhere, anywhere],
        out_specs=anywhere,
        scratch_shapes=[
            pltpu.VMEM((owned, tile, tile), F32),
            pltpu.VMEM((per, tile, tile), F32),
            pltpu.VMEM((2 * slots, tile, tile), BF),
            pltpu.VMEM((places, tile, tile), BF),
            pltpu.VMEM((3, -(-per // 8) * 8, 128), F32),
            pltpu.VMEM((places, tile + 2 * EDGE, width), BF),
            pltpu.VMEM((places, 4 * EDGE, tile), BF),
            pltpu.VMEM((places, 4 * EDGE, tile), BF),
            pltpu.VMEM((2, per, EDGE, tile), BF),
            pltpu.VMEM((2, per, EDGE, tile), BF),
            pltpu.VMEM((per, 4 * EDGE, width), BF),
            pltpu.VMEM((2, slots, 4 * EDGE, width), BF),
            pltpu.VMEM((places, 4 * EDGE, width), BF),
            pltpu.VMEM((PAIRS, chunk, depth), F32),
            pltpu.VMEM((places, PAIRS * chunk, depth), BF),
            pltpu.VMEM((PAIRS * tile, tile), BF),
            pltpu.VMEM((PAIRS * SIDE, tile), BF),
            pltpu.VMEM((places * chunk, PAIRS * tile), BF),
            pltpu.VMEM((places, depth, chunks * SIDE), BF),
            pltpu.VMEM((places * tile, PAIRS * SIDE), BF),
            pltpu.VMEM((chunks, places * chunk, tile), F32),
            pltpu.VMEM((places, tile, tile), BF),
            dma((1 + per,)),
            dma((2,)),
            dma((2,)),
            dma((2,)),
            dma((2,)),
            dma((2,)),
            dma((2,)),
            dma((2,)),
            dma((2,)),
            dma((2 * slots,)),
            dma((2 * slots,)),
            dma((places,)),
        ],
        compiler_params=pltpu.CompilerParams(
            collective_id=0, has_side_effects=True, vmem_limit_bytes=64 * 1024 * 1024
        ),
        name="match",
    )(margin, ccd_first, kernel_coef.T, patches, science)
    return pl.pallas_call(
        functools.partial(mean_kernel, owners, per, owned, slots),
        out_shape=jax.ShapeDtypeStruct(patches.shape, F32),
        in_specs=[smem, anywhere],
        out_specs=anywhere,
        scratch_shapes=[
            pltpu.VMEM(arrived.shape, BF),
            pltpu.VMEM((tile, tile), F32),
            pltpu.VMEM(patches.shape, F32),
            dma(()),
            dma((owned,)),
        ],
        compiler_params=pltpu.CompilerParams(vmem_limit_bytes=64 * 1024 * 1024),
        name="mean",
    )(margin, arrived)


def solution(mesh):
    in_specs = (
        P(("grp", "visit"), None),
        P(("grp", "visit"), None, None),
        P("grp", None),
        P(None, ("grp", "visit")),
        P("grp"),
    )
    out_specs = P(("grp", "visit"), None, None)
    return jax.shard_map(body, mesh=mesh, in_specs=in_specs, out_specs=out_specs, check_vma=False)
```

```python
import functools
import math

import jax
import jax.numpy as jnp
from jax import lax
from jax.experimental import pallas as pl
from jax.experimental.pallas import tpu as pltpu
from jax.sharding import PartitionSpec as P

RADIUS = 10
SIGMAS = 3
ORDERS = 3
PAIRS = SIGMAS * ORDERS
EDGE = 16
SIDE = 128
BF = jnp.bfloat16
F32 = jnp.float32


def sigma_of(g):
    return 0.75 * 2.0**g


def norm_of(g):
    sigma = sigma_of(g)
    return sum(math.exp(-u * u / (2.0 * sigma * sigma)) for u in range(-RADIUS, RADIUS + 1))


def basis_functions(u, g):
    sigma = sigma_of(g)
    inside = jnp.abs(u) <= RADIUS
    base = jnp.where(inside, jnp.exp(u * u * (-1.0 / (2.0 * sigma * sigma))) * (1.0 / norm_of(g)), 0.0)
    scaled = u * (1.0 / sigma)
    first = base * scaled
    return base, first, first * scaled


def named_tiles(margin, strip, owner, owners, per, owned, slots):
    valid = (strip >= 0) & (strip < owners)
    row = (jnp.clip(strip, 0, owners - 1) * per).astype(jnp.int32)
    tiles = [row] * slots
    locals_ = [jnp.int32(0)] * slots
    there = [jnp.int32(0)] * slots
    count = jnp.int32(0)
    for t in range(per):
        patch = margin[0, row + t]
        who = lax.div(patch, jnp.int32(owned))
        named = ((who == owner) & valid).astype(jnp.int32)
        for k in range(slots):
            hit = (named == 1) & (count == k)
            tiles[k] = jnp.where(hit, row + t, tiles[k])
            locals_[k] = jnp.where(hit, patch - who * owned, locals_[k])
            there[k] = jnp.where(hit, jnp.int32(1), there[k])
        count = count + named
    return tiles, locals_, there


def one_hot(size, shift):
    rows = lax.broadcasted_iota(jnp.int32, (size, size), 0)
    cols = lax.broadcasted_iota(jnp.int32, (size, size), 1)
    return jnp.where(((rows - cols + shift) & (size - 1)) == 0, 1.0, 0.0).astype(BF)


def moved(down, x, right):
    a = jnp.dot(down, x, preferred_element_type=F32).astype(BF)
    return jnp.dot(a, right, preferred_element_type=F32).astype(BF)


def match_kernel(
    owners, per, owned, tile, slots,
    margin_h, coef_h, ccd_h, patches_h, science_h,
    out,
    margin, coef, ccd, patches, science, stage, pool, ext, halo, tab, mixed, across, column, diff, parcel, back,
    load_sem, tile_send, tile_recv, halo_send, halo_recv, back_send, back_recv, out_sem,
):
    d = lax.axis_index("visit")
    has_low, has_high = d > 0, d < owners - 1
    low, high = d - 1, d + 1
    chunks = 4
    chunk = tile // chunks
    depth = chunk + 2 * EDGE
    width = tile + SIDE
    places = 3 * slots

    barrier = pltpu.get_barrier_semaphore()

    @pl.when(has_low)
    def _():
        pl.semaphore_signal(barrier, inc=1, device_id={"visit": low}, device_id_type=pl.DeviceIdType.MESH)

    @pl.when(has_high)
    def _():
        pl.semaphore_signal(barrier, inc=1, device_id={"visit": high}, device_id_type=pl.DeviceIdType.MESH)

    patch_load = pltpu.make_async_copy(patches_h, patches, load_sem.at[0])
    science_load = pltpu.make_async_copy(science_h, science, load_sem.at[1])
    margin_load = pltpu.make_async_copy(margin_h, margin, load_sem.at[2])
    coef_load = pltpu.make_async_copy(coef_h, coef, load_sem.at[3])
    ccd_load = pltpu.make_async_copy(ccd_h, ccd, load_sem.at[4])
    margin_load.start()
    patch_load.start()
    coef_load.start()
    ccd_load.start()
    science_load.start()
    margin_load.wait()

    high_tiles, high_local, _ = named_tiles(margin, high, d, owners, per, owned, slots)
    low_tiles, low_local, _ = named_tiles(margin, low, d, owners, per, owned, slots)
    own_tiles, own_local, _ = named_tiles(margin, d, d, owners, per, owned, slots)
    from_low, _, _ = named_tiles(margin, d, low, owners, per, owned, slots)
    from_high, _, _ = named_tiles(margin, d, high, owners, per, owned, slots)

    def remote(src, dst, send, recv, target):
        return pltpu.make_async_remote_copy(
            src_ref=src, dst_ref=dst, send_sem=send, recv_sem=recv,
            device_id={"visit": target}, device_id_type=pl.DeviceIdType.MESH,
        )

    def tile_to_high(k, target):
        return remote(stage.at[k], pool.at[k], tile_send.at[k], tile_recv.at[k], target)

    def tile_to_low(k, target):
        j = slots + k
        return remote(stage.at[j], pool.at[2 * slots + k], tile_send.at[j], tile_recv.at[j], target)

    def aligned(t, local):
        return moved(one_hot(tile, -margin[1, t]), patches[local].astype(BF), one_hot(tile, margin[2, t]))

    patch_load.wait()
    for k in range(slots):
        stage[k] = aligned(high_tiles[k], high_local[k])
        stage[slots + k] = aligned(low_tiles[k], low_local[k])
        if k == 0:
            pl.semaphore_wait(barrier, has_low.astype(jnp.int32) + has_high.astype(jnp.int32))

        @pl.when(has_high)
        def _():
            tile_to_high(k, high).start()

        @pl.when(has_low)
        def _():
            tile_to_low(k, low).start()

    for k in range(slots):
        pool[slots + k] = aligned(own_tiles[k], own_local[k])
    coef_load.wait()
    ccd_load.wait()

    rows = lax.broadcasted_iota(jnp.int32, (chunk, depth), 0)
    cols = lax.broadcasted_iota(jnp.int32, (chunk, depth), 1)
    u = (cols - rows - EDGE).astype(F32)
    for g in range(SIGMAS):
        for v, table in enumerate(basis_functions(u, g)):
            tab[g * ORDERS + v] = table

    def mix_tile(t, carry):
        for g in range(SIGMAS):
            for h in range(ORDERS):
                p = g * ORDERS + h
                total = coef[t, p * ORDERS] * tab[g * ORDERS]
                for v in range(1, ORDERS):
                    total = total + coef[t, p * ORDERS + v] * tab[g * ORDERS + v]
                mixed[t, pl.ds(p * chunk, chunk), :] = total.astype(BF)
        return carry

    lax.fori_loop(0, per, mix_tile, 0)

    def across_rows(b, carry):
        r = lax.broadcasted_iota(jnp.int32, (SIDE, tile), 0)
        c = lax.broadcasted_iota(jnp.int32, (SIDE, tile), 1)
        side = jnp.where(r < SIDE // 2, r + tile, r - SIDE)
        w = (jnp.where(b * SIDE < tile, r + b * SIDE, side) - c).astype(F32)
        for g in range(SIGMAS):
            for h, table in enumerate(basis_functions(w, g)):
                start = pl.multiple_of((g * ORDERS + h) * width + b * SIDE, SIDE)
                across[pl.ds(start, SIDE), :] = table.astype(BF)
        return carry

    lax.fori_loop(0, width // SIDE, across_rows, 0)

    who = [lax.div(margin[0, d * per + t], jnp.int32(owned)) for t in range(per)]
    place = []
    for t in range(per):
        rank = jnp.int32(0)
        for s in range(t):
            rank = rank + (who[s] == who[t]).astype(jnp.int32)
        place.append(jnp.clip((who[t] - d + 1) * slots + rank, 0, places - 1))

    for k in range(slots):

        @pl.when(has_low)
        def _():
            tile_to_high(k, low).wait_recv()

        @pl.when(has_high)
        def _():
            tile_to_low(k, high).wait_recv()

    for t in range(per):
        ext[t, pl.ds(EDGE, tile), pl.ds(0, tile)] = pool[place[t]]

    def halo_to_high(target):
        return remote(
            ext.at[:, pl.ds(tile, EDGE), pl.ds(0, tile)], halo.at[0], halo_send.at[0], halo_recv.at[0], target
        )

    def halo_to_low(target):
        return remote(
            ext.at[:, pl.ds(EDGE, EDGE), pl.ds(0, tile)], halo.at[1], halo_send.at[1], halo_recv.at[1], target
        )

    @pl.when(has_high)
    def _():
        halo_to_high(high).start()

    @pl.when(has_low)
    def _():
        halo_to_low(low).start()

    def fill_sides(first, count):
        lane = lax.broadcasted_iota(jnp.int32, (count, SIDE), 1)
        none = jnp.zeros((count, SIDE), F32)
        for t in range(per):
            right = ext[t + 1, pl.ds(first, count), pl.ds(0, SIDE)].astype(F32) if t + 1 < per else none
            left = ext[t - 1, pl.ds(first, count), pl.ds(tile - SIDE, SIDE)].astype(F32) if t > 0 else none
            ext[t, pl.ds(first, count), pl.ds(tile, SIDE)] = jnp.where(lane < SIDE // 2, right, left).astype(BF)

    fill_sides(EDGE, tile)
    science_load.wait()

    def chunk_to_low(k, c, target):
        at = pl.ds(pl.multiple_of(c * chunk, chunk), chunk)
        return remote(
            parcel.at[k, at], out.at[2 * slots + k, at], back_send.at[c, k], back_recv.at[c, k], target
        )

    def chunk_to_high(k, c, target):
        j = slots + k
        at = pl.ds(pl.multiple_of(c * chunk, chunk), chunk)
        return remote(parcel.at[j, at], out.at[k, at], back_send.at[c, j], back_recv.at[c, j], target)

    def one_chunk(i, carry):
        c = lax.rem(i + 1, chunks)
        at = pl.ds(pl.multiple_of(c * chunk, chunk), chunk)

        @pl.when(i == chunks - 2)
        def _():
            @pl.when(has_low)
            def _():
                halo_to_high(low).wait_recv()

            @pl.when(has_high)
            def _():
                halo_to_low(high).wait_recv()

            keep_top = has_low & (ccd[d] == 0)
            keep_bottom = has_high & (ccd[jnp.minimum(d + 1, owners - 1)] == 0)
            nothing = jnp.zeros((EDGE, tile), BF)
            for t in range(per):
                ext[t, pl.ds(0, EDGE), pl.ds(0, tile)] = jnp.where(keep_top, halo[0, t], nothing)
                ext[t, pl.ds(EDGE + tile, EDGE), pl.ds(0, tile)] = jnp.where(keep_bottom, halo[1, t], nothing)
            fill_sides(0, EDGE)
            fill_sides(EDGE + tile, EDGE)

        window = pl.ds(pl.multiple_of(c * chunk, chunk), depth)
        for t in range(per):
            result = jnp.dot(mixed[t], ext[t, window, :], preferred_element_type=F32).astype(BF)
            for p in range(PAIRS):
                column[pl.ds(t * chunk, chunk), pl.ds(p * width, width)] = result[p * chunk : (p + 1) * chunk]
        matched = jnp.dot(column[...], across[...], preferred_element_type=F32)
        for t in range(per):
            sky = science[at, pl.ds(t * tile, tile)]
            diff[t, at, :] = (sky - matched[t * chunk : (t + 1) * chunk]).astype(BF)
        for k in range(slots):
            parcel[k, at, :] = diff[from_low[k] - d * per, at, :]
            parcel[slots + k, at, :] = diff[from_high[k] - d * per, at, :]

            @pl.when(has_low)
            def _():
                chunk_to_low(k, c, low).start()

            @pl.when(has_high)
            def _():
                chunk_to_high(k, c, high).start()

        return carry

    lax.fori_loop(0, chunks, one_chunk, 0)

    def own_copy(k):
        return pltpu.make_async_copy(back.at[k], out.at[slots + k], out_sem.at[k])

    for k in range(slots):
        t = own_tiles[k]
        back[k] = moved(one_hot(tile, margin[1, t]), diff[t - d * per], one_hot(tile, -margin[2, t]))
        own_copy(k).start()

    @pl.when(has_low)
    def _():
        for k in range(slots):
            tile_to_low(k, low).wait_send()
            for c in range(chunks):
                chunk_to_low(k, c, low).wait_send()
        halo_to_low(low).wait_send()

    @pl.when(has_high)
    def _():
        for k in range(slots):
            tile_to_high(k, high).wait_send()
            for c in range(chunks):
                chunk_to_high(k, c, high).wait_send()
        halo_to_high(high).wait_send()

    for k in range(slots):
        own_copy(k).wait()

    @pl.when(has_low)
    def _():
        for k in range(slots):
            for c in range(chunks):
                chunk_to_high(k, c, low).wait_recv()

    @pl.when(has_high)
    def _():
        for k in range(slots):
            for c in range(chunks):
                chunk_to_low(k, c, high).wait_recv()


def mean_kernel(
    owners, per, owned, slots, margin_h, arrived_h, out_h, margin, arrived, nothing, sums, load_sem, sems
):
    d = lax.axis_index("visit")
    tile = nothing.shape[0]
    margin_load = pltpu.make_async_copy(margin_h, margin, load_sem.at[1])
    margin_load.start()
    load = pltpu.make_async_copy(arrived_h, arrived, load_sem.at[0])
    load.start()
    nothing[...] = jnp.zeros(nothing.shape, F32)
    margin_load.wait()
    tiles, ids, there = [], [], []
    for strip in (d - 1, d, d + 1):
        named, local, present = named_tiles(margin, strip, d, owners, per, owned, slots)
        tiles += named
        ids += local
        there += present

    def count_of(p):
        return sum(((ids[j] == p) & (there[j] == 1)).astype(jnp.int32) for j in range(3 * slots))

    def zero(p, carry):
        @pl.when(count_of(p) == 0)
        def _():
            pltpu.make_async_copy(nothing, out_h.at[p], sems.at[p]).start()

        return carry

    lax.fori_loop(0, owned, zero, 0)
    load.wait()

    for j in list(range(slots, 2 * slots)) + list(range(slots)) + list(range(2 * slots, 3 * slots)):
        order = list(range(slots, 2 * slots)) + list(range(slots)) + list(range(2 * slots, 3 * slots))
        at = order.index(j)
        p = ids[j]
        same = [((ids[i] == p) & (there[i] == 1)).astype(jnp.int32) for i in order]
        before = sum(same[:at], jnp.int32(0))
        after = sum(same[at + 1 :], jnp.int32(0))

        @pl.when(there[j] == 1)
        def _():
            x = arrived[j]
            if not slots <= j < 2 * slots:
                t = tiles[j]
                x = moved(one_hot(tile, margin[1, t]), x, one_hot(tile, -margin[2, t]))
            count = jnp.full((1, 1), before + after + 1, jnp.int32).astype(F32)
            value = x.astype(F32) * (1.0 / count)

            @pl.when(before == 0)
            def _():
                sums[p] = value

            @pl.when(before > 0)
            def _():
                sums[p] += value

            @pl.when(after == 0)
            def _():
                pltpu.make_async_copy(sums.at[p], out_h.at[p], sems.at[p]).start()

    def finish(p, carry):
        pltpu.make_async_copy(sums.at[p], out_h.at[p], sems.at[p]).wait()
        return carry

    lax.fori_loop(0, owned, finish, 0)


def body(science, patches, margin, kernel_coef, ccd_first):
    owners = lax.axis_size("visit")
    owned, tile = patches.shape[0], patches.shape[1]
    per = science.shape[1] // tile
    slots = per // 2
    chunks = 4
    chunk = tile // chunks
    depth = chunk + 2 * EDGE
    width = tile + SIDE
    anywhere = pl.BlockSpec(memory_space=pl.ANY)
    hbm = pl.BlockSpec(memory_space=pltpu.HBM)
    dma = pltpu.SemaphoreType.DMA
    margin = margin.T
    arrived = pl.pallas_call(
        functools.partial(match_kernel, owners, per, owned, tile, slots),
        out_shape=jax.ShapeDtypeStruct((3 * slots, tile, tile), BF),
        in_specs=[hbm] * 5,
        out_specs=anywhere,
        scratch_shapes=[
            pltpu.SMEM(margin.shape, jnp.int32),
            pltpu.SMEM(kernel_coef.shape[::-1], F32),
            pltpu.SMEM(ccd_first.shape, jnp.int32),
            pltpu.VMEM((owned, tile, tile), F32),
            pltpu.VMEM((tile, per * tile), F32),
            pltpu.VMEM((2 * slots, tile, tile), BF),
            pltpu.VMEM((3 * slots, tile, tile), BF),
            pltpu.VMEM((per, tile + 2 * EDGE, width), BF),
            pltpu.VMEM((2, per, EDGE, tile), BF),
            pltpu.VMEM((PAIRS, chunk, depth), F32),
            pltpu.VMEM((per, PAIRS * chunk, depth), BF),
            pltpu.VMEM((PAIRS * width, tile), BF),
            pltpu.VMEM((per * chunk, PAIRS * width), BF),
            pltpu.VMEM((per, tile, tile), BF),
            pltpu.VMEM((2 * slots, tile, tile), BF),
            pltpu.VMEM((slots, tile, tile), BF),
            dma((5,)),
            dma((2 * slots,)),
            dma((2 * slots,)),
            dma((2,)),
            dma((2,)),
            dma((chunks, 2 * slots)),
            dma((chunks, 2 * slots)),
            dma((slots,)),
        ],
        compiler_params=pltpu.CompilerParams(
            collective_id=0, has_side_effects=True, vmem_limit_bytes=64 * 1024 * 1024 - 3 * slots * tile * tile * 2
        ),
        name="match",
    )(margin, kernel_coef.T, ccd_first, patches, science)
    return pl.pallas_call(
        functools.partial(mean_kernel, owners, per, owned, slots),
        out_shape=jax.ShapeDtypeStruct(patches.shape, F32),
        in_specs=[hbm, anywhere],
        out_specs=hbm,
        scratch_shapes=[
            pltpu.SMEM(margin.shape, jnp.int32),
            pltpu.VMEM(arrived.shape, BF),
            pltpu.VMEM((tile, tile), F32),
            pltpu.VMEM(patches.shape, F32),
            dma((2,)),
            dma((owned,)),
        ],
        compiler_params=pltpu.CompilerParams(vmem_limit_bytes=64 * 1024 * 1024 - 3 * slots * tile * tile * 2),
        name="mean",
    )(margin, arrived)


def solution(mesh):
    in_specs = (
        P(("grp", "visit"), None),
        P(("grp", "visit"), None, None),
        P("grp", None),
        P(None, ("grp", "visit")),
        P("grp"),
    )
    out_specs = P(("grp", "visit"), None, None)
    return jax.shard_map(body, mesh=mesh, in_specs=in_specs, out_specs=out_specs, check_vma=False)
```

```python
import functools
import math

import jax
import jax.numpy as jnp
from jax import lax
from jax.experimental import pallas as pl
from jax.experimental.pallas import tpu as pltpu
from jax.sharding import PartitionSpec as P

RADIUS = 10
SIGMAS = 3
ORDERS = 3
PAIRS = SIGMAS * ORDERS
EDGE = 16
SIDE = 128
BF = jnp.bfloat16
F32 = jnp.float32


def sigma_of(g):
    return 0.75 * 2.0**g


def norm_of(g):
    sigma = sigma_of(g)
    return sum(math.exp(-u * u / (2.0 * sigma * sigma)) for u in range(-RADIUS, RADIUS + 1))


def basis_functions(u, g):
    sigma = sigma_of(g)
    inside = jnp.abs(u) <= RADIUS
    base = jnp.where(inside, jnp.exp(u * u * (-1.0 / (2.0 * sigma * sigma))) * (1.0 / norm_of(g)), 0.0)
    scaled = u * (1.0 / sigma)
    first = base * scaled
    return base, first, first * scaled


def named_tiles(margin, strip, owner, owners, per, owned, slots):
    valid = (strip >= 0) & (strip < owners)
    row = (jnp.clip(strip, 0, owners - 1) * per).astype(jnp.int32)
    tiles = [row] * slots
    locals_ = [jnp.int32(0)] * slots
    there = [jnp.int32(0)] * slots
    count = jnp.int32(0)
    for t in range(per):
        patch = margin[0, row + t]
        who = lax.div(patch, jnp.int32(owned))
        named = ((who == owner) & valid).astype(jnp.int32)
        for k in range(slots):
            hit = (named == 1) & (count == k)
            tiles[k] = jnp.where(hit, row + t, tiles[k])
            locals_[k] = jnp.where(hit, patch - who * owned, locals_[k])
            there[k] = jnp.where(hit, jnp.int32(1), there[k])
        count = count + named
    return tiles, locals_, there


def one_hot(size, shift):
    rows = lax.broadcasted_iota(jnp.int32, (size, size), 0)
    cols = lax.broadcasted_iota(jnp.int32, (size, size), 1)
    return jnp.where(((rows - cols + shift) & (size - 1)) == 0, 1.0, 0.0).astype(BF)


def moved(down, x, right):
    a = jnp.dot(down, x, preferred_element_type=F32).astype(BF)
    return jnp.dot(a, right, preferred_element_type=F32).astype(BF)


def match_kernel(
    owners, per, owned, tile, slots,
    margin_h, coef_h, ccd_h, patches_h, science_h,
    out,
    margin, coef, ccd, patches, science, stage, pool, ext, halo, tab, mixed, across, column, diff, parcel, back,
    load_sem, tile_send, tile_recv, halo_send, halo_recv, back_send, back_recv, out_sem,
):
    d = lax.axis_index("visit")
    has_low, has_high = d > 0, d < owners - 1
    low, high = d - 1, d + 1
    chunks = 4
    chunk = tile // chunks
    depth = chunk + 2 * EDGE
    width = tile + SIDE
    places = 3 * slots

    barrier = pltpu.get_barrier_semaphore()

    @pl.when(has_low)
    def _():
        pl.semaphore_signal(barrier, inc=1, device_id={"visit": low}, device_id_type=pl.DeviceIdType.MESH)

    @pl.when(has_high)
    def _():
        pl.semaphore_signal(barrier, inc=1, device_id={"visit": high}, device_id_type=pl.DeviceIdType.MESH)

    patch_load = pltpu.make_async_copy(patches_h, patches, load_sem.at[0])
    science_load = pltpu.make_async_copy(science_h, science, load_sem.at[1])
    margin_load = pltpu.make_async_copy(margin_h, margin, load_sem.at[2])
    coef_load = pltpu.make_async_copy(coef_h, coef, load_sem.at[3])
    ccd_load = pltpu.make_async_copy(ccd_h, ccd, load_sem.at[4])
    margin_load.start()
    patch_load.start()
    coef_load.start()
    ccd_load.start()
    science_load.start()
    margin_load.wait()

    high_tiles, high_local, _ = named_tiles(margin, high, d, owners, per, owned, slots)
    low_tiles, low_local, _ = named_tiles(margin, low, d, owners, per, owned, slots)
    own_tiles, own_local, _ = named_tiles(margin, d, d, owners, per, owned, slots)
    from_low, _, _ = named_tiles(margin, d, low, owners, per, owned, slots)
    from_high, _, _ = named_tiles(margin, d, high, owners, per, owned, slots)

    def remote(src, dst, send, recv, target):
        return pltpu.make_async_remote_copy(
            src_ref=src, dst_ref=dst, send_sem=send, recv_sem=recv,
            device_id={"visit": target}, device_id_type=pl.DeviceIdType.MESH,
        )

    def tile_to_high(k, target):
        return remote(stage.at[k], pool.at[k], tile_send.at[k], tile_recv.at[k], target)

    def tile_to_low(k, target):
        j = slots + k
        return remote(stage.at[j], pool.at[2 * slots + k], tile_send.at[j], tile_recv.at[j], target)

    def aligned(t, local):
        return moved(one_hot(tile, -margin[1, t]), patches[local].astype(BF), one_hot(tile, margin[2, t]))

    rows = lax.broadcasted_iota(jnp.int32, (chunk, depth), 0)
    cols = lax.broadcasted_iota(jnp.int32, (chunk, depth), 1)
    u = (cols - rows - EDGE).astype(F32)
    for g in range(SIGMAS):
        for v, table in enumerate(basis_functions(u, g)):
            tab[g * ORDERS + v] = table

    def across_rows(b, carry):
        r = lax.broadcasted_iota(jnp.int32, (SIDE, tile), 0)
        c = lax.broadcasted_iota(jnp.int32, (SIDE, tile), 1)
        side = jnp.where(r < SIDE // 2, r + tile, r - SIDE)
        w = (jnp.where(b * SIDE < tile, r + b * SIDE, side) - c).astype(F32)
        for g in range(SIGMAS):
            for h, table in enumerate(basis_functions(w, g)):
                start = pl.multiple_of((g * ORDERS + h) * width + b * SIDE, SIDE)
                across[pl.ds(start, SIDE), :] = table.astype(BF)
        return carry

    lax.fori_loop(0, width // SIDE, across_rows, 0)

    patch_load.wait()
    for k in range(slots):
        stage[k] = aligned(high_tiles[k], high_local[k])
        stage[slots + k] = aligned(low_tiles[k], low_local[k])
        if k == 0:
            pl.semaphore_wait(barrier, has_low.astype(jnp.int32) + has_high.astype(jnp.int32))

        @pl.when(has_high)
        def _():
            tile_to_high(k, high).start()

        @pl.when(has_low)
        def _():
            tile_to_low(k, low).start()

    for k in range(slots):
        pool[slots + k] = aligned(own_tiles[k], own_local[k])
    coef_load.wait()
    ccd_load.wait()

    def mix_tile(t, carry):
        for g in range(SIGMAS):
            for h in range(ORDERS):
                p = g * ORDERS + h
                total = coef[t, p * ORDERS] * tab[g * ORDERS]
                for v in range(1, ORDERS):
                    total = total + coef[t, p * ORDERS + v] * tab[g * ORDERS + v]
                mixed[t, pl.ds(p * chunk, chunk), :] = total.astype(BF)
        return carry

    lax.fori_loop(0, per, mix_tile, 0)

    who = [lax.div(margin[0, d * per + t], jnp.int32(owned)) for t in range(per)]
    place = []
    for t in range(per):
        rank = jnp.int32(0)
        for s in range(t):
            rank = rank + (who[s] == who[t]).astype(jnp.int32)
        place.append(jnp.clip((who[t] - d + 1) * slots + rank, 0, places - 1))

    for k in range(slots):

        @pl.when(has_low)
        def _():
            tile_to_high(k, low).wait_recv()

        @pl.when(has_high)
        def _():
            tile_to_low(k, high).wait_recv()

    for t in range(per):
        ext[t, pl.ds(EDGE, tile), pl.ds(0, tile)] = pool[place[t]]

    def halo_to_high(target):
        return remote(
            ext.at[:, pl.ds(tile, EDGE), pl.ds(0, tile)], halo.at[0], halo_send.at[0], halo_recv.at[0], target
        )

    def halo_to_low(target):
        return remote(
            ext.at[:, pl.ds(EDGE, EDGE), pl.ds(0, tile)], halo.at[1], halo_send.at[1], halo_recv.at[1], target
        )

    @pl.when(has_high)
    def _():
        halo_to_high(high).start()

    @pl.when(has_low)
    def _():
        halo_to_low(low).start()

    def fill_sides(first, count):
        lane = lax.broadcasted_iota(jnp.int32, (count, SIDE), 1)
        none = jnp.zeros((count, SIDE), F32)
        for t in range(per):
            right = ext[t + 1, pl.ds(first, count), pl.ds(0, SIDE)].astype(F32) if t + 1 < per else none
            left = ext[t - 1, pl.ds(first, count), pl.ds(tile - SIDE, SIDE)].astype(F32) if t > 0 else none
            ext[t, pl.ds(first, count), pl.ds(tile, SIDE)] = jnp.where(lane < SIDE // 2, right, left).astype(BF)

    fill_sides(EDGE, tile)
    science_load.wait()

    def chunk_to_low(k, c, target):
        at = pl.ds(pl.multiple_of(c * chunk, chunk), chunk)
        return remote(
            parcel.at[k, at], out.at[2 * slots + k, at], back_send.at[c, k], back_recv.at[c, k], target
        )

    def chunk_to_high(k, c, target):
        j = slots + k
        at = pl.ds(pl.multiple_of(c * chunk, chunk), chunk)
        return remote(parcel.at[j, at], out.at[k, at], back_send.at[c, j], back_recv.at[c, j], target)

    def one_chunk(i, carry):
        c = lax.rem(i + 1, chunks)
        at = pl.ds(pl.multiple_of(c * chunk, chunk), chunk)

        @pl.when(i == chunks - 2)
        def _():
            @pl.when(has_low)
            def _():
                halo_to_high(low).wait_recv()

            @pl.when(has_high)
            def _():
                halo_to_low(high).wait_recv()

            keep_top = has_low & (ccd[d] == 0)
            keep_bottom = has_high & (ccd[jnp.minimum(d + 1, owners - 1)] == 0)
            nothing = jnp.zeros((EDGE, tile), BF)
            for t in range(per):
                ext[t, pl.ds(0, EDGE), pl.ds(0, tile)] = jnp.where(keep_top, halo[0, t], nothing)
                ext[t, pl.ds(EDGE + tile, EDGE), pl.ds(0, tile)] = jnp.where(keep_bottom, halo[1, t], nothing)
            fill_sides(0, EDGE)
            fill_sides(EDGE + tile, EDGE)

        window = pl.ds(pl.multiple_of(c * chunk, chunk), depth)
        for t in range(per):
            result = jnp.dot(mixed[t], ext[t, window, :], preferred_element_type=F32).astype(BF)
            for p in range(PAIRS):
                column[pl.ds(t * chunk, chunk), pl.ds(p * width, width)] = result[p * chunk : (p + 1) * chunk]
        matched = jnp.dot(column[...], across[...], preferred_element_type=F32)
        for t in range(per):
            sky = science[at, pl.ds(t * tile, tile)]
            diff[t, at, :] = (sky - matched[t * chunk : (t + 1) * chunk]).astype(BF)
        for k in range(slots):
            parcel[k, at, :] = diff[from_low[k] - d * per, at, :]
            parcel[slots + k, at, :] = diff[from_high[k] - d * per, at, :]

            @pl.when(has_low)
            def _():
                chunk_to_low(k, c, low).start()

            @pl.when(has_high)
            def _():
                chunk_to_high(k, c, high).start()

        return carry

    lax.fori_loop(0, chunks, one_chunk, 0)

    def own_copy(k):
        return pltpu.make_async_copy(back.at[k], out.at[slots + k], out_sem.at[k])

    for k in range(slots):
        t = own_tiles[k]
        back[k] = moved(one_hot(tile, margin[1, t]), diff[t - d * per], one_hot(tile, -margin[2, t]))
        own_copy(k).start()

    @pl.when(has_low)
    def _():
        for k in range(slots):
            tile_to_low(k, low).wait_send()
            for c in range(chunks):
                chunk_to_low(k, c, low).wait_send()
        halo_to_low(low).wait_send()

    @pl.when(has_high)
    def _():
        for k in range(slots):
            tile_to_high(k, high).wait_send()
            for c in range(chunks):
                chunk_to_high(k, c, high).wait_send()
        halo_to_high(high).wait_send()

    for k in range(slots):
        own_copy(k).wait()

    @pl.when(has_low)
    def _():
        for k in range(slots):
            for c in range(chunks):
                chunk_to_high(k, c, low).wait_recv()

    @pl.when(has_high)
    def _():
        for k in range(slots):
            for c in range(chunks):
                chunk_to_low(k, c, high).wait_recv()


def mean_kernel(
    owners, per, owned, slots,
    margin_h, arrived_h, out_h,
    margin, arrived, nothing, sums, down, right, load_sem, sems,
):
    d = lax.axis_index("visit")
    tile = nothing.shape[0]
    margin_load = pltpu.make_async_copy(margin_h, margin, load_sem.at[1])
    margin_load.start()
    load = pltpu.make_async_copy(arrived_h, arrived, load_sem.at[0])
    load.start()
    nothing[...] = jnp.zeros(nothing.shape, F32)
    margin_load.wait()
    tiles, ids, there = [], [], []
    for strip in (d - 1, d, d + 1):
        named, local, present = named_tiles(margin, strip, d, owners, per, owned, slots)
        tiles += named
        ids += local
        there += present

    def count_of(p):
        return sum(((ids[j] == p) & (there[j] == 1)).astype(jnp.int32) for j in range(3 * slots))

    def zero(p, carry):
        @pl.when(count_of(p) == 0)
        def _():
            pltpu.make_async_copy(nothing, out_h.at[p], sems.at[p]).start()

        return carry

    lax.fori_loop(0, owned, zero, 0)
    for i, j in enumerate(list(range(slots)) + list(range(2 * slots, 3 * slots))):
        down[i] = one_hot(tile, margin[1, tiles[j]])
        right[i] = one_hot(tile, -margin[2, tiles[j]])
    load.wait()

    for j in list(range(slots, 2 * slots)) + list(range(slots)) + list(range(2 * slots, 3 * slots)):
        order = list(range(slots, 2 * slots)) + list(range(slots)) + list(range(2 * slots, 3 * slots))
        at = order.index(j)
        p = ids[j]
        same = [((ids[i] == p) & (there[i] == 1)).astype(jnp.int32) for i in order]
        before = sum(same[:at], jnp.int32(0))
        after = sum(same[at + 1 :], jnp.int32(0))

        @pl.when(there[j] == 1)
        def _():
            x = arrived[j]
            if not slots <= j < 2 * slots:
                i = j if j < slots else j - slots
                x = moved(down[i], x, right[i])
            count = jnp.full((1, 1), before + after + 1, jnp.int32).astype(F32)
            value = x.astype(F32) * (1.0 / count)

            @pl.when(before == 0)
            def _():
                sums[p] = value

            @pl.when(before > 0)
            def _():
                sums[p] += value

            @pl.when(after == 0)
            def _():
                pltpu.make_async_copy(sums.at[p], out_h.at[p], sems.at[p]).start()

    def finish(p, carry):
        pltpu.make_async_copy(sums.at[p], out_h.at[p], sems.at[p]).wait()
        return carry

    lax.fori_loop(0, owned, finish, 0)


def body(science, patches, margin, kernel_coef, ccd_first):
    owners = lax.axis_size("visit")
    owned, tile = patches.shape[0], patches.shape[1]
    per = science.shape[1] // tile
    slots = per // 2
    chunks = 4
    chunk = tile // chunks
    depth = chunk + 2 * EDGE
    width = tile + SIDE
    anywhere = pl.BlockSpec(memory_space=pl.ANY)
    hbm = pl.BlockSpec(memory_space=pltpu.HBM)
    dma = pltpu.SemaphoreType.DMA
    margin = margin.T
    arrived = pl.pallas_call(
        functools.partial(match_kernel, owners, per, owned, tile, slots),
        out_shape=jax.ShapeDtypeStruct((3 * slots, tile, tile), BF),
        in_specs=[hbm] * 5,
        out_specs=anywhere,
        scratch_shapes=[
            pltpu.SMEM(margin.shape, jnp.int32),
            pltpu.SMEM(kernel_coef.shape[::-1], F32),
            pltpu.SMEM(ccd_first.shape, jnp.int32),
            pltpu.VMEM((owned, tile, tile), F32),
            pltpu.VMEM((tile, per * tile), F32),
            pltpu.VMEM((2 * slots, tile, tile), BF),
            pltpu.VMEM((3 * slots, tile, tile), BF),
            pltpu.VMEM((per, tile + 2 * EDGE, width), BF),
            pltpu.VMEM((2, per, EDGE, tile), BF),
            pltpu.VMEM((PAIRS, chunk, depth), F32),
            pltpu.VMEM((per, PAIRS * chunk, depth), BF),
            pltpu.VMEM((PAIRS * width, tile), BF),
            pltpu.VMEM((per * chunk, PAIRS * width), BF),
            pltpu.VMEM((per, tile, tile), BF),
            pltpu.VMEM((2 * slots, tile, tile), BF),
            pltpu.VMEM((slots, tile, tile), BF),
            dma((5,)),
            dma((2 * slots,)),
            dma((2 * slots,)),
            dma((2,)),
            dma((2,)),
            dma((chunks, 2 * slots)),
            dma((chunks, 2 * slots)),
            dma((slots,)),
        ],
        compiler_params=pltpu.CompilerParams(
            collective_id=0, has_side_effects=True, vmem_limit_bytes=64 * 1024 * 1024 - 3 * slots * tile * tile * 2
        ),
        name="match",
    )(margin, kernel_coef.T, ccd_first, patches, science)
    return pl.pallas_call(
        functools.partial(mean_kernel, owners, per, owned, slots),
        out_shape=jax.ShapeDtypeStruct(patches.shape, F32),
        in_specs=[hbm, anywhere],
        out_specs=hbm,
        scratch_shapes=[
            pltpu.SMEM(margin.shape, jnp.int32),
            pltpu.VMEM(arrived.shape, BF),
            pltpu.VMEM((tile, tile), F32),
            pltpu.VMEM(patches.shape, F32),
            pltpu.VMEM((2 * slots, tile, tile), BF),
            pltpu.VMEM((2 * slots, tile, tile), BF),
            dma((2,)),
            dma((owned,)),
        ],
        compiler_params=pltpu.CompilerParams(vmem_limit_bytes=64 * 1024 * 1024 - 3 * slots * tile * tile * 2),
        name="mean",
    )(margin, arrived)


def solution(mesh):
    in_specs = (
        P(("grp", "visit"), None),
        P(("grp", "visit"), None, None),
        P("grp", None),
        P(None, ("grp", "visit")),
        P("grp"),
    )
    out_specs = P(("grp", "visit"), None, None)
    return jax.shard_map(body, mesh=mesh, in_specs=in_specs, out_specs=out_specs, check_vma=False)
```

```python
import functools
import math

import jax
import jax.numpy as jnp
from jax import lax
from jax.experimental import pallas as pl
from jax.experimental.pallas import tpu as pltpu
from jax.sharding import PartitionSpec as P

RADIUS = 10
SIGMAS = 3
ORDERS = 3
PAIRS = SIGMAS * ORDERS
EDGE = 16
SIDE = 128
BF = jnp.bfloat16
F32 = jnp.float32


def sigma_of(g):
    return 0.75 * 2.0**g


def norm_of(g):
    sigma = sigma_of(g)
    return sum(math.exp(-u * u / (2.0 * sigma * sigma)) for u in range(-RADIUS, RADIUS + 1))


def basis_functions(u, g):
    sigma = sigma_of(g)
    inside = jnp.abs(u) <= RADIUS
    base = jnp.where(inside, jnp.exp(u * u * (-1.0 / (2.0 * sigma * sigma))) * (1.0 / norm_of(g)), 0.0)
    scaled = u * (1.0 / sigma)
    first = base * scaled
    return base, first, first * scaled


def named_tiles(margin, strip, owner, owners, per, owned, slots):
    valid = (strip >= 0) & (strip < owners)
    row = (jnp.clip(strip, 0, owners - 1) * per).astype(jnp.int32)
    tiles = [row] * slots
    locals_ = [jnp.int32(0)] * slots
    there = [jnp.int32(0)] * slots
    count = jnp.int32(0)
    for t in range(per):
        patch = margin[0, row + t]
        who = lax.div(patch, jnp.int32(owned))
        named = ((who == owner) & valid).astype(jnp.int32)
        for k in range(slots):
            hit = (named == 1) & (count == k)
            tiles[k] = jnp.where(hit, row + t, tiles[k])
            locals_[k] = jnp.where(hit, patch - who * owned, locals_[k])
            there[k] = jnp.where(hit, jnp.int32(1), there[k])
        count = count + named
    return tiles, locals_, there


def one_hot(size, shift):
    rows = lax.broadcasted_iota(jnp.int32, (size, size), 0)
    cols = lax.broadcasted_iota(jnp.int32, (size, size), 1)
    return jnp.where(((rows - cols + shift) & (size - 1)) == 0, 1.0, 0.0).astype(BF)


def moved(down, x, right):
    a = jnp.dot(down, x, preferred_element_type=F32).astype(BF)
    return jnp.dot(a, right, preferred_element_type=F32).astype(BF)


def match_kernel(
    owners, per, owned, tile, slots,
    margin_h, coef_h, ccd_h, patches_h, science_h,
    out,
    margin, coef, ccd, patches, science, stage, early, late, ext, halo_out, halo, tab, mixed, across, across_side,
    column, side_column, matched, diff, parcel, back,
    load_sem, tile_send, tile_recv, halo_send, halo_recv, back_send, back_recv, out_sem,
):
    d = lax.axis_index("visit")
    has_low, has_high = d > 0, d < owners - 1
    low, high = d - 1, d + 1
    chunks = 4
    chunk = tile // chunks
    depth = chunk + 2 * EDGE
    width = tile + SIDE

    barrier = pltpu.get_barrier_semaphore()

    @pl.when(has_low)
    def _():
        pl.semaphore_signal(barrier, inc=1, device_id={"visit": low}, device_id_type=pl.DeviceIdType.MESH)

    @pl.when(has_high)
    def _():
        pl.semaphore_signal(barrier, inc=1, device_id={"visit": high}, device_id_type=pl.DeviceIdType.MESH)

    patch_load = pltpu.make_async_copy(patches_h, patches, load_sem.at[0])
    science_loads = [
        pltpu.make_async_copy(science_h.at[:, pl.ds(t * tile, tile)], science.at[t], load_sem.at[4 + t])
        for t in range(per)
    ]
    margin_load = pltpu.make_async_copy(margin_h, margin, load_sem.at[2])
    coef_load = pltpu.make_async_copy(coef_h, coef, load_sem.at[1])
    ccd_load = pltpu.make_async_copy(ccd_h, ccd, load_sem.at[3])
    margin_load.start()
    patch_load.start()
    coef_load.start()
    ccd_load.start()
    for load in science_loads:
        load.start()
    margin_load.wait()

    high_tiles, high_local, _ = named_tiles(margin, high, d, owners, per, owned, slots)
    low_tiles, low_local, _ = named_tiles(margin, low, d, owners, per, owned, slots)
    own_tiles, own_local, _ = named_tiles(margin, d, d, owners, per, owned, slots)
    from_low, _, _ = named_tiles(margin, d, low, owners, per, owned, slots)
    from_high, _, _ = named_tiles(margin, d, high, owners, per, owned, slots)

    def remote(src, dst, send, recv, target):
        return pltpu.make_async_remote_copy(
            src_ref=src, dst_ref=dst, send_sem=send, recv_sem=recv,
            device_id={"visit": target}, device_id_type=pl.DeviceIdType.MESH,
        )

    def tile_to_high(k, target):
        dst = early.at[0] if k == 0 else late.at[k - 1]
        return remote(stage.at[k], dst, tile_send.at[k], tile_recv.at[k], target)

    def tile_to_low(k, target):
        j = slots + k
        dst = early.at[slots + 1] if k == 0 else late.at[slots + k - 2]
        return remote(stage.at[j], dst, tile_send.at[j], tile_recv.at[j], target)

    def aligned(t, local):
        return moved(one_hot(tile, -margin[1, t]), patches[local].astype(BF), one_hot(tile, margin[2, t]))

    rows = lax.broadcasted_iota(jnp.int32, (chunk, depth), 0)
    cols = lax.broadcasted_iota(jnp.int32, (chunk, depth), 1)
    u = (cols - rows - EDGE).astype(F32)
    for g in range(SIGMAS):
        for v, table in enumerate(basis_functions(u, g)):
            tab[g * ORDERS + v] = table

    def across_rows(b, carry):
        r = lax.broadcasted_iota(jnp.int32, (SIDE, tile), 0)
        c = lax.broadcasted_iota(jnp.int32, (SIDE, tile), 1)
        side = jnp.where(r < SIDE // 2, r + tile, r - SIDE)
        main = b * SIDE < tile
        w = (jnp.where(main, r + b * SIDE, side) - c).astype(F32)
        for g in range(SIGMAS):
            for h, table in enumerate(basis_functions(w, g)):
                p = g * ORDERS + h
                table = table.astype(BF)

                @pl.when(main)
                def _():
                    across[pl.ds(pl.multiple_of(p * tile + b * SIDE, SIDE), SIDE), :] = table

                @pl.when(jnp.logical_not(main))
                def _():
                    across_side[pl.ds(p * SIDE, SIDE), :] = table

        return carry

    lax.fori_loop(0, width // SIDE, across_rows, 0)

    patch_load.wait()
    for k in range(slots):
        stage[k] = aligned(high_tiles[k], high_local[k])
        stage[slots + k] = aligned(low_tiles[k], low_local[k])
        if k == 0:
            pl.semaphore_wait(barrier, has_low.astype(jnp.int32) + has_high.astype(jnp.int32))

        @pl.when(has_high)
        def _():
            tile_to_high(k, high).start()

        @pl.when(has_low)
        def _():
            tile_to_low(k, low).start()

    for k in range(slots):
        early[1 + k] = aligned(own_tiles[k], own_local[k])
    coef_load.wait()
    ccd_load.wait()

    who = [lax.div(margin[0, d * per + t], jnp.int32(owned)) for t in range(per)]
    ranks = [sum([(who[s] == who[t]).astype(jnp.int32) for s in range(t)], jnp.int32(0)) for t in range(per)]
    keys = [jnp.where(who[t] == d, 0, 1 + ranks[t]) for t in range(per)]
    position = []
    for t in range(per):
        ahead = [(keys[s] <= keys[t]) if s < t else (keys[s] < keys[t]) for s in range(per) if s != t]
        position.append(sum([x.astype(jnp.int32) for x in ahead], jnp.int32(0)))

    def at_position(values, q):
        return sum([jnp.where(position[t] == q, values[t], 0) for t in range(per)], jnp.int32(0))

    order = [at_position(list(range(per)), q) for q in range(per)]
    is_late = [at_position([(keys[t] > 1).astype(jnp.int32) for t in range(per)], q) for q in range(per)]
    side = [who[t] - d for t in range(per)]
    early_place = [
        jnp.where(side[t] == 0, 1 + ranks[t], jnp.where(side[t] < 0, 0, slots + 1)) for t in range(per)
    ]
    late_place = [jnp.maximum(ranks[t] - 1, 0) + jnp.where(side[t] < 0, 0, slots - 1) for t in range(per)]
    early_at = [jnp.clip(at_position(early_place, q), 0, slots + 1) for q in range(per)]
    late_at = [jnp.clip(at_position(late_place, q), 0, 2 * slots - 3) for q in range(per)]
    right_at, left_at = [], []
    for q in range(per):
        right_at.append(sum([jnp.where(order[q] == t - 1, position[t], 0) for t in range(1, per)], jnp.int32(0)))
        left_at.append(sum([jnp.where(order[q] == t + 1, position[t], 0) for t in range(per - 1)], jnp.int32(0)))

    def mix_tile(q, carry):
        t = order[0]
        for i in range(1, per):
            t = jnp.where(q == i, order[i], t)
        for g in range(SIGMAS):
            for h in range(ORDERS):
                p = g * ORDERS + h
                total = coef[t, p * ORDERS] * tab[g * ORDERS]
                for v in range(1, ORDERS):
                    total = total + coef[t, p * ORDERS + v] * tab[g * ORDERS + v]
                mixed[q, pl.ds(p * chunk, chunk), :] = total.astype(BF)
        return carry

    lax.fori_loop(0, per, mix_tile, 0)

    def tiles_arrive(k):
        @pl.when(has_low)
        def _():
            tile_to_high(k, low).wait_recv()

        @pl.when(has_high)
        def _():
            tile_to_low(k, high).wait_recv()

    def down_columns(q, c, at):
        window = pl.ds(pl.multiple_of(c * chunk, chunk), depth)
        result = jnp.dot(mixed[q], ext[q, window, pl.ds(0, tile)], preferred_element_type=F32).astype(BF)
        for p in range(PAIRS):
            column[pl.ds(at * chunk, chunk), pl.ds(p * tile, tile)] = result[p * chunk : (p + 1) * chunk]

    half = per // 2
    tiles_arrive(0)

    def middle(first):
        for q in range(half):
            for i in range(2):
                down_columns(first + q, 1 + i, 2 * q + i)
        result = jnp.dot(column[...], across[...], preferred_element_type=F32)
        for q in range(half):
            matched[first + q, pl.ds(chunk, 2 * chunk), :] = result[2 * q * chunk : 2 * (q + 1) * chunk]

    for q in range(half):
        ext[q, pl.ds(EDGE, tile), pl.ds(0, tile)] = early[early_at[q]]
    middle(0)
    for k in range(1, slots):
        tiles_arrive(k)
    for q in range(half, per):
        x = jnp.where(is_late[q] == 1, late[late_at[q]].astype(F32), early[early_at[q]].astype(F32)).astype(BF)
        ext[q, pl.ds(EDGE, tile), pl.ds(0, tile)] = x

    def halo_to_high(target):
        return remote(halo_out.at[0], halo.at[0], halo_send.at[0], halo_recv.at[0], target)

    def halo_to_low(target):
        return remote(halo_out.at[1], halo.at[1], halo_send.at[1], halo_recv.at[1], target)

    for t in range(per):
        halo_out[0, t] = ext[position[t], pl.ds(tile, EDGE), pl.ds(0, tile)]
        halo_out[1, t] = ext[position[t], pl.ds(EDGE, EDGE), pl.ds(0, tile)]

    @pl.when(has_high)
    def _():
        halo_to_high(high).start()

    @pl.when(has_low)
    def _():
        halo_to_low(low).start()

    def fill_sides(first, count):
        lane = lax.broadcasted_iota(jnp.int32, (count, SIDE), 1)
        none = jnp.zeros((count, SIDE), F32)
        for q in range(per):
            right = ext[right_at[q], pl.ds(first, count), pl.ds(0, SIDE)].astype(F32)
            left = ext[left_at[q], pl.ds(first, count), pl.ds(tile - SIDE, SIDE)].astype(F32)
            right = jnp.where(order[q] + 1 < per, right, none)
            left = jnp.where(order[q] > 0, left, none)
            ext[q, pl.ds(first, count), pl.ds(tile, SIDE)] = jnp.where(lane < SIDE // 2, right, left).astype(BF)

    fill_sides(EDGE, tile)
    middle(half)
    for load in science_loads:
        load.wait()

    def chunk_to_low(k, c, target):
        at = pl.ds(pl.multiple_of(c * chunk, chunk), chunk)
        return remote(
            parcel.at[k, at], out.at[2 * slots + k, at], back_send.at[c, k], back_recv.at[c, k], target
        )

    def chunk_to_high(k, c, target):
        j = slots + k
        at = pl.ds(pl.multiple_of(c * chunk, chunk), chunk)
        return remote(parcel.at[j, at], out.at[k, at], back_send.at[c, j], back_recv.at[c, j], target)

    def position_of(t):
        return sum([jnp.where(t - d * per == s, position[s], 0) for s in range(per)], jnp.int32(0))

    def one_chunk(i, carry):
        c = lax.rem(i + 1, chunks)
        at = pl.ds(pl.multiple_of(c * chunk, chunk), chunk)

        @pl.when(i == chunks - 2)
        def _():
            @pl.when(has_low)
            def _():
                halo_to_high(low).wait_recv()

            @pl.when(has_high)
            def _():
                halo_to_low(high).wait_recv()

            keep_top = has_low & (ccd[d] == 0)
            keep_bottom = has_high & (ccd[jnp.minimum(d + 1, owners - 1)] == 0)
            nothing = jnp.zeros((EDGE, tile), BF)
            for t in range(per):
                top = jnp.where(keep_top, halo[0, order[t]], nothing)
                bottom = jnp.where(keep_bottom, halo[1, order[t]], nothing)
                ext[t, pl.ds(0, EDGE), pl.ds(0, tile)] = top
                ext[t, pl.ds(EDGE + tile, EDGE), pl.ds(0, tile)] = bottom
            fill_sides(0, EDGE)
            fill_sides(EDGE + tile, EDGE)

        @pl.when(i >= chunks - 2)
        def _():
            for q in range(per):
                down_columns(q, c, q)
            result = jnp.dot(column[...], across[...], preferred_element_type=F32)
            for q in range(per):
                matched[q, at, :] = result[q * chunk : (q + 1) * chunk]

        window = pl.ds(pl.multiple_of(c * chunk, chunk), depth)
        for q in range(per):
            result = jnp.dot(
                mixed[q], ext[q, window, pl.ds(tile, SIDE)], preferred_element_type=F32
            ).astype(BF)
            for p in range(PAIRS):
                side_column[pl.ds(q * chunk, chunk), pl.ds(p * SIDE, SIDE)] = result[p * chunk : (p + 1) * chunk]
        sides = jnp.dot(side_column[...], across_side[...], preferred_element_type=F32)
        for q in range(per):
            sky = science[order[q], at, :]
            diff[q, at, :] = (sky - (matched[q, at, :] + sides[q * chunk : (q + 1) * chunk])).astype(BF)
        for k in range(slots):
            parcel[k, at, :] = diff[position_of(from_low[k]), at, :]
            parcel[slots + k, at, :] = diff[position_of(from_high[k]), at, :]

            @pl.when(has_low)
            def _():
                chunk_to_low(k, c, low).start()

            @pl.when(has_high)
            def _():
                chunk_to_high(k, c, high).start()

        return carry

    lax.fori_loop(0, chunks, one_chunk, 0)

    def own_copy(k):
        return pltpu.make_async_copy(back.at[k], out.at[slots + k], out_sem.at[k])

    for k in range(slots):
        t = own_tiles[k]
        back[k] = moved(one_hot(tile, margin[1, t]), diff[position_of(t)], one_hot(tile, -margin[2, t]))
        own_copy(k).start()

    @pl.when(has_low)
    def _():
        for k in range(slots):
            tile_to_low(k, low).wait_send()
            for c in range(chunks):
                chunk_to_low(k, c, low).wait_send()
        halo_to_low(low).wait_send()

    @pl.when(has_high)
    def _():
        for k in range(slots):
            tile_to_high(k, high).wait_send()
            for c in range(chunks):
                chunk_to_high(k, c, high).wait_send()
        halo_to_high(high).wait_send()

    for k in range(slots):
        own_copy(k).wait()

    @pl.when(has_low)
    def _():
        for k in range(slots):
            for c in range(chunks):
                chunk_to_high(k, c, low).wait_recv()

    @pl.when(has_high)
    def _():
        for k in range(slots):
            for c in range(chunks):
                chunk_to_low(k, c, high).wait_recv()


def mean_kernel(
    owners, per, owned, slots,
    margin_h, arrived_h, out_h,
    margin, arrived, nothing, sums, down, right, load_sem, sems,
):
    d = lax.axis_index("visit")
    tile = nothing.shape[0]
    margin_load = pltpu.make_async_copy(margin_h, margin, load_sem.at[1])
    margin_load.start()
    load = pltpu.make_async_copy(arrived_h, arrived, load_sem.at[0])
    load.start()
    nothing[...] = jnp.zeros(nothing.shape, F32)
    margin_load.wait()
    tiles, ids, there = [], [], []
    for strip in (d - 1, d, d + 1):
        named, local, present = named_tiles(margin, strip, d, owners, per, owned, slots)
        tiles += named
        ids += local
        there += present

    def count_of(p):
        return sum(((ids[j] == p) & (there[j] == 1)).astype(jnp.int32) for j in range(3 * slots))

    def zero(p, carry):
        @pl.when(count_of(p) == 0)
        def _():
            pltpu.make_async_copy(nothing, out_h.at[p], sems.at[p]).start()

        return carry

    lax.fori_loop(0, owned, zero, 0)
    for i, j in enumerate(list(range(slots)) + list(range(2 * slots, 3 * slots))):
        down[i] = one_hot(tile, margin[1, tiles[j]])
        right[i] = one_hot(tile, -margin[2, tiles[j]])
    load.wait()

    for j in list(range(slots, 2 * slots)) + list(range(slots)) + list(range(2 * slots, 3 * slots)):
        order = list(range(slots, 2 * slots)) + list(range(slots)) + list(range(2 * slots, 3 * slots))
        at = order.index(j)
        p = ids[j]
        same = [((ids[i] == p) & (there[i] == 1)).astype(jnp.int32) for i in order]
        before = sum(same[:at], jnp.int32(0))
        after = sum(same[at + 1 :], jnp.int32(0))

        @pl.when(there[j] == 1)
        def _():
            x = arrived[j]
            if not slots <= j < 2 * slots:
                i = j if j < slots else j - slots
                x = moved(down[i], x, right[i])
            count = jnp.full((1, 1), before + after + 1, jnp.int32).astype(F32)
            value = x.astype(F32) * (1.0 / count)

            @pl.when(before == 0)
            def _():
                sums[p] = value

            @pl.when(before > 0)
            def _():
                sums[p] += value

            @pl.when(after == 0)
            def _():
                pltpu.make_async_copy(sums.at[p], out_h.at[p], sems.at[p]).start()

    def finish(p, carry):
        pltpu.make_async_copy(sums.at[p], out_h.at[p], sems.at[p]).wait()
        return carry

    lax.fori_loop(0, owned, finish, 0)


def body(science, patches, margin, kernel_coef, ccd_first):
    owners = lax.axis_size("visit")
    owned, tile = patches.shape[0], patches.shape[1]
    per = science.shape[1] // tile
    slots = per // 2
    chunks = 4
    chunk = tile // chunks
    depth = chunk + 2 * EDGE
    width = tile + SIDE
    anywhere = pl.BlockSpec(memory_space=pl.ANY)
    hbm = pl.BlockSpec(memory_space=pltpu.HBM)
    dma = pltpu.SemaphoreType.DMA
    margin = margin.T
    arrived = pl.pallas_call(
        functools.partial(match_kernel, owners, per, owned, tile, slots),
        out_shape=jax.ShapeDtypeStruct((3 * slots, tile, tile), BF),
        in_specs=[hbm] * 5,
        out_specs=anywhere,
        scratch_shapes=[
            pltpu.SMEM(margin.shape, jnp.int32),
            pltpu.SMEM(kernel_coef.shape[::-1], F32),
            pltpu.SMEM(ccd_first.shape, jnp.int32),
            pltpu.VMEM((owned, tile, tile), F32),
            pltpu.VMEM((per, tile, tile), F32),
            pltpu.VMEM((2 * slots, tile, tile), BF),
            pltpu.VMEM((slots + 2, tile, tile), BF),
            pltpu.VMEM((2 * slots - 2, tile, tile), BF),
            pltpu.VMEM((per, tile + 2 * EDGE, width), BF),
            pltpu.VMEM((2, per, EDGE, tile), BF),
            pltpu.VMEM((2, per, EDGE, tile), BF),
            pltpu.VMEM((PAIRS, chunk, depth), F32),
            pltpu.VMEM((per, PAIRS * chunk, depth), BF),
            pltpu.VMEM((PAIRS * tile, tile), BF),
            pltpu.VMEM((PAIRS * SIDE, tile), BF),
            pltpu.VMEM((per * chunk, PAIRS * tile), BF),
            pltpu.VMEM((per * chunk, PAIRS * SIDE), BF),
            pltpu.VMEM((per, tile, tile), F32),
            pltpu.VMEM((per, tile, tile), BF),
            pltpu.VMEM((2 * slots, tile, tile), BF),
            pltpu.VMEM((slots, tile, tile), BF),
            dma((4 + per,)),
            dma((2 * slots,)),
            dma((2 * slots,)),
            dma((2,)),
            dma((2,)),
            dma((chunks, 2 * slots)),
            dma((chunks, 2 * slots)),
            dma((slots,)),
        ],
        compiler_params=pltpu.CompilerParams(
            collective_id=0, has_side_effects=True, vmem_limit_bytes=64 * 1024 * 1024 - 3 * slots * tile * tile * 2
        ),
        name="match",
    )(margin, kernel_coef.T, ccd_first, patches, science)
    return pl.pallas_call(
        functools.partial(mean_kernel, owners, per, owned, slots),
        out_shape=jax.ShapeDtypeStruct(patches.shape, F32),
        in_specs=[hbm, anywhere],
        out_specs=hbm,
        scratch_shapes=[
            pltpu.SMEM(margin.shape, jnp.int32),
            pltpu.VMEM(arrived.shape, BF),
            pltpu.VMEM((tile, tile), F32),
            pltpu.VMEM(patches.shape, F32),
            pltpu.VMEM((2 * slots, tile, tile), BF),
            pltpu.VMEM((2 * slots, tile, tile), BF),
            dma((2,)),
            dma((owned,)),
        ],
        compiler_params=pltpu.CompilerParams(vmem_limit_bytes=64 * 1024 * 1024 - 3 * slots * tile * tile * 2),
        name="mean",
    )(margin, arrived)


def solution(mesh):
    in_specs = (
        P(("grp", "visit"), None),
        P(("grp", "visit"), None, None),
        P("grp", None),
        P(None, ("grp", "visit")),
        P("grp"),
    )
    out_specs = P(("grp", "visit"), None, None)
    return jax.shard_map(body, mesh=mesh, in_specs=in_specs, out_specs=out_specs, check_vma=False)
```

```python
import functools
import math

import jax
import jax.numpy as jnp
from jax import lax
from jax.experimental import pallas as pl
from jax.experimental.pallas import tpu as pltpu
from jax.sharding import PartitionSpec as P

RADIUS = 10
SIGMAS = 3
ORDERS = 3
PAIRS = SIGMAS * ORDERS
EDGE = 16
SIDE = 128
BF = jnp.bfloat16
F32 = jnp.float32


def sigma_of(g):
    return 0.75 * 2.0**g


def norm_of(g):
    sigma = sigma_of(g)
    return sum(math.exp(-u * u / (2.0 * sigma * sigma)) for u in range(-RADIUS, RADIUS + 1))


def basis_functions(u, g):
    sigma = sigma_of(g)
    inside = jnp.abs(u) <= RADIUS
    base = jnp.where(inside, jnp.exp(u * u * (-1.0 / (2.0 * sigma * sigma))) * (1.0 / norm_of(g)), 0.0)
    scaled = u * (1.0 / sigma)
    first = base * scaled
    return base, first, first * scaled


def named_tiles(margin, strip, owner, owners, per, owned, slots):
    valid = (strip >= 0) & (strip < owners)
    row = (jnp.clip(strip, 0, owners - 1) * per).astype(jnp.int32)
    tiles = [row] * slots
    locals_ = [jnp.int32(0)] * slots
    there = [jnp.int32(0)] * slots
    count = jnp.int32(0)
    for t in range(per):
        patch = margin[0, row + t]
        who = lax.div(patch, jnp.int32(owned))
        named = ((who == owner) & valid).astype(jnp.int32)
        for k in range(slots):
            hit = (named == 1) & (count == k)
            tiles[k] = jnp.where(hit, row + t, tiles[k])
            locals_[k] = jnp.where(hit, patch - who * owned, locals_[k])
            there[k] = jnp.where(hit, jnp.int32(1), there[k])
        count = count + named
    return tiles, locals_, there


def one_hot(size, shift):
    rows = lax.broadcasted_iota(jnp.int32, (size, size), 0)
    cols = lax.broadcasted_iota(jnp.int32, (size, size), 1)
    return jnp.where(((rows - cols + shift) & (size - 1)) == 0, 1.0, 0.0).astype(BF)


def moved(down, x, right):
    a = jnp.dot(down, x, preferred_element_type=F32).astype(BF)
    return jnp.dot(a, right, preferred_element_type=F32).astype(BF)


def match_kernel(
    owners, per, owned, tile, slots,
    margin_h, coef_h, ccd_h, patches_h, science_h,
    out,
    margin, coef, ccd, patches, science, stage, early, late, ext, halo_out, halo, tab, mixed, across, across_side,
    column, side_column, matched, diff, parcel, back,
    load_sem, tile_send, tile_recv, halo_send, halo_recv, back_send, back_recv, out_sem,
):
    d = lax.axis_index("visit")
    has_low, has_high = d > 0, d < owners - 1
    low, high = d - 1, d + 1
    chunks = 4
    chunk = tile // chunks
    depth = chunk + 2 * EDGE
    width = tile + SIDE

    barrier = pltpu.get_barrier_semaphore()

    @pl.when(has_low)
    def _():
        pl.semaphore_signal(barrier, inc=1, device_id={"visit": low}, device_id_type=pl.DeviceIdType.MESH)

    @pl.when(has_high)
    def _():
        pl.semaphore_signal(barrier, inc=1, device_id={"visit": high}, device_id_type=pl.DeviceIdType.MESH)

    patch_load = pltpu.make_async_copy(patches_h, patches, load_sem.at[0])
    science_loads = [
        pltpu.make_async_copy(science_h.at[:, pl.ds(t * tile, tile)], science.at[t], load_sem.at[4 + t])
        for t in range(per)
    ]
    margin_load = pltpu.make_async_copy(margin_h, margin, load_sem.at[2])
    coef_load = pltpu.make_async_copy(coef_h, coef, load_sem.at[1])
    ccd_load = pltpu.make_async_copy(ccd_h, ccd, load_sem.at[3])
    margin_load.start()
    patch_load.start()
    coef_load.start()
    ccd_load.start()
    margin_load.wait()

    high_tiles, high_local, _ = named_tiles(margin, high, d, owners, per, owned, slots)
    low_tiles, low_local, _ = named_tiles(margin, low, d, owners, per, owned, slots)
    own_tiles, own_local, _ = named_tiles(margin, d, d, owners, per, owned, slots)
    from_low, _, _ = named_tiles(margin, d, low, owners, per, owned, slots)
    from_high, _, _ = named_tiles(margin, d, high, owners, per, owned, slots)

    def remote(src, dst, send, recv, target):
        return pltpu.make_async_remote_copy(
            src_ref=src, dst_ref=dst, send_sem=send, recv_sem=recv,
            device_id={"visit": target}, device_id_type=pl.DeviceIdType.MESH,
        )

    def tile_to_high(k, target, src=0):
        dst = early.at[0] if k == 0 else late.at[k - 1]
        return remote(stage.at[src + k], dst, tile_send.at[k], tile_recv.at[k], target)

    def tile_to_low(k, target, src=0):
        j = slots + k
        dst = early.at[slots + 1] if k == 0 else late.at[slots + k - 2]
        return remote(stage.at[src + k], dst, tile_send.at[j], tile_recv.at[j], target)

    def aligned(t, local):
        return moved(one_hot(tile, -margin[1, t]), patches[local].astype(BF), one_hot(tile, margin[2, t]))

    patch_load.wait()
    for load in science_loads:
        load.start()

    odd = lax.rem(d, 2) == 1
    for part in range(2):
        up = odd if part == 0 else jnp.logical_not(odd)
        for k in range(slots):
            t = jnp.where(up, high_tiles[k], low_tiles[k])
            local = jnp.where(up, high_local[k], low_local[k])
            src = part * slots
            stage[src + k] = aligned(t, local)
            if part == 0 and k == 0:
                pl.semaphore_wait(barrier, has_low.astype(jnp.int32) + has_high.astype(jnp.int32))

            @pl.when(up & has_high)
            def _():
                tile_to_high(k, high, src).start()

            @pl.when(jnp.logical_not(up) & has_low)
            def _():
                tile_to_low(k, low, src).start()

    for k in range(slots):
        early[1 + k] = aligned(own_tiles[k], own_local[k])
    coef_load.wait()
    ccd_load.wait()

    rows = lax.broadcasted_iota(jnp.int32, (chunk, depth), 0)
    cols = lax.broadcasted_iota(jnp.int32, (chunk, depth), 1)
    u = (cols - rows - EDGE).astype(F32)
    for g in range(SIGMAS):
        for v, table in enumerate(basis_functions(u, g)):
            tab[g * ORDERS + v] = table

    def across_rows(b, carry):
        r = lax.broadcasted_iota(jnp.int32, (SIDE, tile), 0)
        c = lax.broadcasted_iota(jnp.int32, (SIDE, tile), 1)
        side = jnp.where(r < SIDE // 2, r + tile, r - SIDE)
        main = b * SIDE < tile
        w = (jnp.where(main, r + b * SIDE, side) - c).astype(F32)
        for g in range(SIGMAS):
            for h, table in enumerate(basis_functions(w, g)):
                p = g * ORDERS + h
                table = table.astype(BF)

                @pl.when(main)
                def _():
                    across[pl.ds(pl.multiple_of(p * tile + b * SIDE, SIDE), SIDE), :] = table

                @pl.when(jnp.logical_not(main))
                def _():
                    across_side[pl.ds(p * SIDE, SIDE), :] = table

        return carry

    lax.fori_loop(0, width // SIDE, across_rows, 0)

    who = [lax.div(margin[0, d * per + t], jnp.int32(owned)) for t in range(per)]
    ranks = [sum([(who[s] == who[t]).astype(jnp.int32) for s in range(t)], jnp.int32(0)) for t in range(per)]
    keys = [jnp.where(who[t] == d, 0, 1 + ranks[t]) for t in range(per)]
    position = []
    for t in range(per):
        ahead = [(keys[s] <= keys[t]) if s < t else (keys[s] < keys[t]) for s in range(per) if s != t]
        position.append(sum([x.astype(jnp.int32) for x in ahead], jnp.int32(0)))

    def at_position(values, q):
        return sum([jnp.where(position[t] == q, values[t], 0) for t in range(per)], jnp.int32(0))

    order = [at_position(list(range(per)), q) for q in range(per)]
    is_late = [at_position([(keys[t] > 1).astype(jnp.int32) for t in range(per)], q) for q in range(per)]
    side = [who[t] - d for t in range(per)]
    early_place = [
        jnp.where(side[t] == 0, 1 + ranks[t], jnp.where(side[t] < 0, 0, slots + 1)) for t in range(per)
    ]
    late_place = [jnp.maximum(ranks[t] - 1, 0) + jnp.where(side[t] < 0, 0, slots - 1) for t in range(per)]
    early_at = [jnp.clip(at_position(early_place, q), 0, slots + 1) for q in range(per)]
    late_at = [jnp.clip(at_position(late_place, q), 0, 2 * slots - 3) for q in range(per)]
    right_at, left_at = [], []
    for q in range(per):
        right_at.append(sum([jnp.where(order[q] == t - 1, position[t], 0) for t in range(1, per)], jnp.int32(0)))
        left_at.append(sum([jnp.where(order[q] == t + 1, position[t], 0) for t in range(per - 1)], jnp.int32(0)))

    def mix_tile(q, carry):
        t = order[0]
        for i in range(1, per):
            t = jnp.where(q == i, order[i], t)
        for g in range(SIGMAS):
            for h in range(ORDERS):
                p = g * ORDERS + h
                total = coef[t, p * ORDERS] * tab[g * ORDERS]
                for v in range(1, ORDERS):
                    total = total + coef[t, p * ORDERS + v] * tab[g * ORDERS + v]
                mixed[q, pl.ds(p * chunk, chunk), :] = total.astype(BF)
        return carry

    lax.fori_loop(0, per, mix_tile, 0)

    def tiles_arrive(k):
        @pl.when(has_low)
        def _():
            tile_to_high(k, low).wait_recv()

        @pl.when(has_high)
        def _():
            tile_to_low(k, high).wait_recv()

    def down_columns(q, c, at):
        window = pl.ds(pl.multiple_of(c * chunk, chunk), depth)
        result = jnp.dot(mixed[q], ext[q, window, pl.ds(0, tile)], preferred_element_type=F32).astype(BF)
        for p in range(PAIRS):
            column[pl.ds(at * chunk, chunk), pl.ds(p * tile, tile)] = result[p * chunk : (p + 1) * chunk]

    half = per // 2
    tiles_arrive(0)

    def middle(first):
        for q in range(half):
            for i in range(2):
                down_columns(first + q, 1 + i, 2 * q + i)
        result = jnp.dot(column[...], across[...], preferred_element_type=F32)
        for q in range(half):
            matched[first + q, pl.ds(chunk, 2 * chunk), :] = result[2 * q * chunk : 2 * (q + 1) * chunk]

    for q in range(half):
        ext[q, pl.ds(EDGE, tile), pl.ds(0, tile)] = early[early_at[q]]
    middle(0)
    for k in range(1, slots):
        tiles_arrive(k)
    for q in range(half, per):
        x = jnp.where(is_late[q] == 1, late[late_at[q]].astype(F32), early[early_at[q]].astype(F32)).astype(BF)
        ext[q, pl.ds(EDGE, tile), pl.ds(0, tile)] = x

    def halo_to_high(target):
        return remote(halo_out.at[0], halo.at[0], halo_send.at[0], halo_recv.at[0], target)

    def halo_to_low(target):
        return remote(halo_out.at[1], halo.at[1], halo_send.at[1], halo_recv.at[1], target)

    for t in range(per):
        halo_out[0, t] = ext[position[t], pl.ds(tile, EDGE), pl.ds(0, tile)]
        halo_out[1, t] = ext[position[t], pl.ds(EDGE, EDGE), pl.ds(0, tile)]

    @pl.when(has_high)
    def _():
        halo_to_high(high).start()

    @pl.when(has_low)
    def _():
        halo_to_low(low).start()

    def fill_sides(first, count):
        lane = lax.broadcasted_iota(jnp.int32, (count, SIDE), 1)
        none = jnp.zeros((count, SIDE), F32)
        for q in range(per):
            right = ext[right_at[q], pl.ds(first, count), pl.ds(0, SIDE)].astype(F32)
            left = ext[left_at[q], pl.ds(first, count), pl.ds(tile - SIDE, SIDE)].astype(F32)
            right = jnp.where(order[q] + 1 < per, right, none)
            left = jnp.where(order[q] > 0, left, none)
            ext[q, pl.ds(first, count), pl.ds(tile, SIDE)] = jnp.where(lane < SIDE // 2, right, left).astype(BF)

    fill_sides(EDGE, tile)
    middle(half)
    for load in science_loads:
        load.wait()

    def chunk_to_low(k, c, target):
        at = pl.ds(pl.multiple_of(c * chunk, chunk), chunk)
        return remote(
            parcel.at[k, at], out.at[2 * slots + k, at], back_send.at[c, k], back_recv.at[c, k], target
        )

    def chunk_to_high(k, c, target):
        j = slots + k
        at = pl.ds(pl.multiple_of(c * chunk, chunk), chunk)
        return remote(parcel.at[j, at], out.at[k, at], back_send.at[c, j], back_recv.at[c, j], target)

    def position_of(t):
        return sum([jnp.where(t - d * per == s, position[s], 0) for s in range(per)], jnp.int32(0))

    def one_chunk(i, carry):
        c = lax.rem(i + 1, chunks)
        at = pl.ds(pl.multiple_of(c * chunk, chunk), chunk)

        @pl.when(i == chunks - 2)
        def _():
            @pl.when(has_low)
            def _():
                halo_to_high(low).wait_recv()

            @pl.when(has_high)
            def _():
                halo_to_low(high).wait_recv()

            keep_top = has_low & (ccd[d] == 0)
            keep_bottom = has_high & (ccd[jnp.minimum(d + 1, owners - 1)] == 0)
            nothing = jnp.zeros((EDGE, tile), BF)
            for t in range(per):
                top = jnp.where(keep_top, halo[0, order[t]], nothing)
                bottom = jnp.where(keep_bottom, halo[1, order[t]], nothing)
                ext[t, pl.ds(0, EDGE), pl.ds(0, tile)] = top
                ext[t, pl.ds(EDGE + tile, EDGE), pl.ds(0, tile)] = bottom
            fill_sides(0, EDGE)
            fill_sides(EDGE + tile, EDGE)

        @pl.when(i >= chunks - 2)
        def _():
            for q in range(per):
                down_columns(q, c, q)
            result = jnp.dot(column[...], across[...], preferred_element_type=F32)
            for q in range(per):
                matched[q, at, :] = result[q * chunk : (q + 1) * chunk]

        window = pl.ds(pl.multiple_of(c * chunk, chunk), depth)
        for q in range(per):
            result = jnp.dot(
                mixed[q], ext[q, window, pl.ds(tile, SIDE)], preferred_element_type=F32
            ).astype(BF)
            for p in range(PAIRS):
                side_column[pl.ds(q * chunk, chunk), pl.ds(p * SIDE, SIDE)] = result[p * chunk : (p + 1) * chunk]
        sides = jnp.dot(side_column[...], across_side[...], preferred_element_type=F32)
        for q in range(per):
            sky = science[order[q], at, :]
            diff[q, at, :] = (sky - (matched[q, at, :] + sides[q * chunk : (q + 1) * chunk])).astype(BF)
        for k in range(slots):
            parcel[k, at, :] = diff[position_of(from_low[k]), at, :]
            parcel[slots + k, at, :] = diff[position_of(from_high[k]), at, :]

            @pl.when(has_low)
            def _():
                chunk_to_low(k, c, low).start()

            @pl.when(has_high)
            def _():
                chunk_to_high(k, c, high).start()

        return carry

    lax.fori_loop(0, chunks, one_chunk, 0)

    def own_copy(k):
        return pltpu.make_async_copy(back.at[k], out.at[slots + k], out_sem.at[k])

    for k in range(slots):
        t = own_tiles[k]
        back[k] = moved(one_hot(tile, margin[1, t]), diff[position_of(t)], one_hot(tile, -margin[2, t]))
        own_copy(k).start()

    @pl.when(has_low)
    def _():
        for k in range(slots):
            tile_to_low(k, low).wait_send()
            for c in range(chunks):
                chunk_to_low(k, c, low).wait_send()
        halo_to_low(low).wait_send()

    @pl.when(has_high)
    def _():
        for k in range(slots):
            tile_to_high(k, high).wait_send()
            for c in range(chunks):
                chunk_to_high(k, c, high).wait_send()
        halo_to_high(high).wait_send()

    for k in range(slots):
        own_copy(k).wait()

    @pl.when(has_low)
    def _():
        for k in range(slots):
            for c in range(chunks):
                chunk_to_high(k, c, low).wait_recv()

    @pl.when(has_high)
    def _():
        for k in range(slots):
            for c in range(chunks):
                chunk_to_low(k, c, high).wait_recv()


def mean_kernel(
    owners, per, owned, slots,
    margin_h, arrived_h, out_h,
    margin, arrived, nothing, sums, down, right, load_sem, sems,
):
    d = lax.axis_index("visit")
    tile = nothing.shape[0]
    margin_load = pltpu.make_async_copy(margin_h, margin, load_sem.at[1])
    margin_load.start()
    load = pltpu.make_async_copy(arrived_h, arrived, load_sem.at[0])
    load.start()
    nothing[...] = jnp.zeros(nothing.shape, F32)
    margin_load.wait()
    tiles, ids, there = [], [], []
    for strip in (d - 1, d, d + 1):
        named, local, present = named_tiles(margin, strip, d, owners, per, owned, slots)
        tiles += named
        ids += local
        there += present

    def count_of(p):
        return sum(((ids[j] == p) & (there[j] == 1)).astype(jnp.int32) for j in range(3 * slots))

    def zero(p, carry):
        @pl.when(count_of(p) == 0)
        def _():
            pltpu.make_async_copy(nothing, out_h.at[p], sems.at[p]).start()

        return carry

    lax.fori_loop(0, owned, zero, 0)
    for i, j in enumerate(list(range(slots)) + list(range(2 * slots, 3 * slots))):
        down[i] = one_hot(tile, margin[1, tiles[j]])
        right[i] = one_hot(tile, -margin[2, tiles[j]])
    load.wait()

    for j in list(range(slots, 2 * slots)) + list(range(slots)) + list(range(2 * slots, 3 * slots)):
        order = list(range(slots, 2 * slots)) + list(range(slots)) + list(range(2 * slots, 3 * slots))
        at = order.index(j)
        p = ids[j]
        same = [((ids[i] == p) & (there[i] == 1)).astype(jnp.int32) for i in order]
        before = sum(same[:at], jnp.int32(0))
        after = sum(same[at + 1 :], jnp.int32(0))

        @pl.when(there[j] == 1)
        def _():
            x = arrived[j]
            if not slots <= j < 2 * slots:
                i = j if j < slots else j - slots
                x = moved(down[i], x, right[i])
            count = jnp.full((1, 1), before + after + 1, jnp.int32).astype(F32)
            value = x.astype(F32) * (1.0 / count)

            @pl.when(before == 0)
            def _():
                sums[p] = value

            @pl.when(before > 0)
            def _():
                sums[p] += value

            @pl.when(after == 0)
            def _():
                pltpu.make_async_copy(sums.at[p], out_h.at[p], sems.at[p]).start()

    def finish(p, carry):
        pltpu.make_async_copy(sums.at[p], out_h.at[p], sems.at[p]).wait()
        return carry

    lax.fori_loop(0, owned, finish, 0)


def body(science, patches, margin, kernel_coef, ccd_first):
    owners = lax.axis_size("visit")
    owned, tile = patches.shape[0], patches.shape[1]
    per = science.shape[1] // tile
    slots = per // 2
    chunks = 4
    chunk = tile // chunks
    depth = chunk + 2 * EDGE
    width = tile + SIDE
    anywhere = pl.BlockSpec(memory_space=pl.ANY)
    hbm = pl.BlockSpec(memory_space=pltpu.HBM)
    dma = pltpu.SemaphoreType.DMA
    margin = margin.T
    arrived = pl.pallas_call(
        functools.partial(match_kernel, owners, per, owned, tile, slots),
        out_shape=jax.ShapeDtypeStruct((3 * slots, tile, tile), BF),
        in_specs=[hbm] * 5,
        out_specs=anywhere,
        scratch_shapes=[
            pltpu.SMEM(margin.shape, jnp.int32),
            pltpu.SMEM(kernel_coef.shape[::-1], F32),
            pltpu.SMEM(ccd_first.shape, jnp.int32),
            pltpu.VMEM((owned, tile, tile), F32),
            pltpu.VMEM((per, tile, tile), F32),
            pltpu.VMEM((2 * slots, tile, tile), BF),
            pltpu.VMEM((slots + 2, tile, tile), BF),
            pltpu.VMEM((2 * slots - 2, tile, tile), BF),
            pltpu.VMEM((per, tile + 2 * EDGE, width), BF),
            pltpu.VMEM((2, per, EDGE, tile), BF),
            pltpu.VMEM((2, per, EDGE, tile), BF),
            pltpu.VMEM((PAIRS, chunk, depth), F32),
            pltpu.VMEM((per, PAIRS * chunk, depth), BF),
            pltpu.VMEM((PAIRS * tile, tile), BF),
            pltpu.VMEM((PAIRS * SIDE, tile), BF),
            pltpu.VMEM((per * chunk, PAIRS * tile), BF),
            pltpu.VMEM((per * chunk, PAIRS * SIDE), BF),
            pltpu.VMEM((per, tile, tile), F32),
            pltpu.VMEM((per, tile, tile), BF),
            pltpu.VMEM((2 * slots, tile, tile), BF),
            pltpu.VMEM((slots, tile, tile), BF),
            dma((4 + per,)),
            dma((2 * slots,)),
            dma((2 * slots,)),
            dma((2,)),
            dma((2,)),
            dma((chunks, 2 * slots)),
            dma((chunks, 2 * slots)),
            dma((slots,)),
        ],
        compiler_params=pltpu.CompilerParams(
            collective_id=0, has_side_effects=True, vmem_limit_bytes=64 * 1024 * 1024 - 3 * slots * tile * tile * 2
        ),
        name="match",
    )(margin, kernel_coef.T, ccd_first, patches, science)
    return pl.pallas_call(
        functools.partial(mean_kernel, owners, per, owned, slots),
        out_shape=jax.ShapeDtypeStruct(patches.shape, F32),
        in_specs=[hbm, anywhere],
        out_specs=hbm,
        scratch_shapes=[
            pltpu.SMEM(margin.shape, jnp.int32),
            pltpu.VMEM(arrived.shape, BF),
            pltpu.VMEM((tile, tile), F32),
            pltpu.VMEM(patches.shape, F32),
            pltpu.VMEM((2 * slots, tile, tile), BF),
            pltpu.VMEM((2 * slots, tile, tile), BF),
            dma((2,)),
            dma((owned,)),
        ],
        compiler_params=pltpu.CompilerParams(vmem_limit_bytes=64 * 1024 * 1024 - 3 * slots * tile * tile * 2),
        name="mean",
    )(margin, arrived)


def solution(mesh):
    in_specs = (
        P(("grp", "visit"), None),
        P(("grp", "visit"), None, None),
        P("grp", None),
        P(None, ("grp", "visit")),
        P("grp"),
    )
    out_specs = P(("grp", "visit"), None, None)
    return jax.shard_map(body, mesh=mesh, in_specs=in_specs, out_specs=out_specs, check_vma=False)
```

```python
import functools
import math

import jax
import jax.numpy as jnp
from jax import lax
from jax.experimental import pallas as pl
from jax.experimental.pallas import tpu as pltpu
from jax.sharding import PartitionSpec as P

RADIUS = 10
SIGMAS = 3
ORDERS = 3
PAIRS = SIGMAS * ORDERS
EDGE = 16
SIDE = 128
BF = jnp.bfloat16
F32 = jnp.float32


def sigma_of(g):
    return 0.75 * 2.0**g


def norm_of(g):
    sigma = sigma_of(g)
    return sum(math.exp(-u * u / (2.0 * sigma * sigma)) for u in range(-RADIUS, RADIUS + 1))


def basis_functions(u, g):
    sigma = sigma_of(g)
    inside = jnp.abs(u) <= RADIUS
    base = jnp.where(inside, jnp.exp(u * u * (-1.0 / (2.0 * sigma * sigma))) * (1.0 / norm_of(g)), 0.0)
    scaled = u * (1.0 / sigma)
    first = base * scaled
    return base, first, first * scaled


def named_tiles(margin, strip, owner, owners, per, owned, slots):
    valid = (strip >= 0) & (strip < owners)
    row = (jnp.clip(strip, 0, owners - 1) * per).astype(jnp.int32)
    tiles = [row] * slots
    locals_ = [jnp.int32(0)] * slots
    there = [jnp.int32(0)] * slots
    count = jnp.int32(0)
    for t in range(per):
        patch = margin[0, row + t]
        who = lax.div(patch, jnp.int32(owned))
        named = ((who == owner) & valid).astype(jnp.int32)
        for k in range(slots):
            hit = (named == 1) & (count == k)
            tiles[k] = jnp.where(hit, row + t, tiles[k])
            locals_[k] = jnp.where(hit, patch - who * owned, locals_[k])
            there[k] = jnp.where(hit, jnp.int32(1), there[k])
        count = count + named
    return tiles, locals_, there


def one_hot(size, shift):
    rows = lax.broadcasted_iota(jnp.int32, (size, size), 0)
    cols = lax.broadcasted_iota(jnp.int32, (size, size), 1)
    return jnp.where(((rows - cols + shift) & (size - 1)) == 0, 1.0, 0.0).astype(BF)


def moved(down, x, right):
    a = jnp.dot(down, x, preferred_element_type=F32).astype(BF)
    return jnp.dot(a, right, preferred_element_type=F32).astype(BF)


def match_kernel(
    owners, per, owned, tile, slots,
    margin_h, coef_h, ccd_h, patches_h, science_h,
    out,
    margin, coef, ccd, patches, science, stage, early, late, ext, halo_out, halo, tab, mixed, across, across_side,
    column, side_column, matched, diff, parcel, back,
    load_sem, tile_send, tile_recv, halo_send, halo_recv, back_send, back_recv, out_sem,
):
    d = lax.axis_index("visit")
    has_low, has_high = d > 0, d < owners - 1
    low, high = d - 1, d + 1
    chunks = 4
    chunk = tile // chunks
    depth = chunk + 2 * EDGE
    width = tile + SIDE

    barrier = pltpu.get_barrier_semaphore()

    @pl.when(has_low)
    def _():
        pl.semaphore_signal(barrier, inc=1, device_id={"visit": low}, device_id_type=pl.DeviceIdType.MESH)

    @pl.when(has_high)
    def _():
        pl.semaphore_signal(barrier, inc=1, device_id={"visit": high}, device_id_type=pl.DeviceIdType.MESH)

    patch_load = pltpu.make_async_copy(patches_h, patches, load_sem.at[0])
    science_loads = [
        pltpu.make_async_copy(science_h.at[:, pl.ds(t * tile, tile)], science.at[t], load_sem.at[4 + t])
        for t in range(per)
    ]
    margin_load = pltpu.make_async_copy(margin_h, margin, load_sem.at[2])
    coef_load = pltpu.make_async_copy(coef_h, coef, load_sem.at[1])
    ccd_load = pltpu.make_async_copy(ccd_h, ccd, load_sem.at[3])
    margin_load.start()
    patch_load.start()
    coef_load.start()
    ccd_load.start()
    margin_load.wait()

    high_tiles, high_local, _ = named_tiles(margin, high, d, owners, per, owned, slots)
    low_tiles, low_local, _ = named_tiles(margin, low, d, owners, per, owned, slots)
    own_tiles, own_local, _ = named_tiles(margin, d, d, owners, per, owned, slots)
    from_low, _, _ = named_tiles(margin, d, low, owners, per, owned, slots)
    from_high, _, _ = named_tiles(margin, d, high, owners, per, owned, slots)

    def remote(src, dst, send, recv, target):
        return pltpu.make_async_remote_copy(
            src_ref=src, dst_ref=dst, send_sem=send, recv_sem=recv,
            device_id={"visit": target}, device_id_type=pl.DeviceIdType.MESH,
        )

    def tile_to_high(k, target, src=0):
        dst = early.at[0] if k == 0 else late.at[k - 1]
        return remote(stage.at[src + k], dst, tile_send.at[k], tile_recv.at[k], target)

    def tile_to_low(k, target, src=0):
        j = slots + k
        dst = early.at[slots + 1] if k == 0 else late.at[slots + k - 2]
        return remote(stage.at[src + k], dst, tile_send.at[j], tile_recv.at[j], target)

    def aligned(t, local):
        return moved(one_hot(tile, -margin[1, t]), patches[local].astype(BF), one_hot(tile, margin[2, t]))

    patch_load.wait()
    for load in science_loads:
        load.start()

    odd = lax.rem(d, 2) == 1
    for part in range(2):
        up = odd if part == 0 else jnp.logical_not(odd)
        for k in range(slots):
            t = jnp.where(up, high_tiles[k], low_tiles[k])
            local = jnp.where(up, high_local[k], low_local[k])
            src = part * slots
            stage[src + k] = aligned(t, local)
            if part == 0 and k == 0:
                pl.semaphore_wait(barrier, has_low.astype(jnp.int32) + has_high.astype(jnp.int32))

            @pl.when(up & has_high)
            def _():
                tile_to_high(k, high, src).start()

            @pl.when(jnp.logical_not(up) & has_low)
            def _():
                tile_to_low(k, low, src).start()

    for k in range(slots):
        early[1 + k] = aligned(own_tiles[k], own_local[k])
    coef_load.wait()
    ccd_load.wait()

    rows = lax.broadcasted_iota(jnp.int32, (chunk, depth), 0)
    cols = lax.broadcasted_iota(jnp.int32, (chunk, depth), 1)
    u = (cols - rows - EDGE).astype(F32)
    for g in range(SIGMAS):
        for v, table in enumerate(basis_functions(u, g)):
            tab[g * ORDERS + v] = table

    def across_rows(b, carry):
        r = lax.broadcasted_iota(jnp.int32, (SIDE, tile), 0)
        c = lax.broadcasted_iota(jnp.int32, (SIDE, tile), 1)
        side = jnp.where(r < SIDE // 2, r + tile, r - SIDE)
        main = b * SIDE < tile
        w = (jnp.where(main, r + b * SIDE, side) - c).astype(F32)
        for g in range(SIGMAS):
            for h, table in enumerate(basis_functions(w, g)):
                p = g * ORDERS + h
                table = table.astype(BF)

                @pl.when(main)
                def _():
                    across[pl.ds(pl.multiple_of(p * tile + b * SIDE, SIDE), SIDE), :] = table

                @pl.when(jnp.logical_not(main))
                def _():
                    across_side[pl.ds(p * SIDE, SIDE), :] = table

        return carry

    lax.fori_loop(0, width // SIDE, across_rows, 0)

    who = [lax.div(margin[0, d * per + t], jnp.int32(owned)) for t in range(per)]
    ranks = [sum([(who[s] == who[t]).astype(jnp.int32) for s in range(t)], jnp.int32(0)) for t in range(per)]
    keys = [jnp.where(who[t] == d, 0, 1 + ranks[t]) for t in range(per)]
    position = []
    for t in range(per):
        ahead = [(keys[s] <= keys[t]) if s < t else (keys[s] < keys[t]) for s in range(per) if s != t]
        position.append(sum([x.astype(jnp.int32) for x in ahead], jnp.int32(0)))

    def at_position(values, q):
        return sum([jnp.where(position[t] == q, values[t], 0) for t in range(per)], jnp.int32(0))

    order = [at_position(list(range(per)), q) for q in range(per)]
    is_late = [at_position([(keys[t] > 1).astype(jnp.int32) for t in range(per)], q) for q in range(per)]
    side = [who[t] - d for t in range(per)]
    early_place = [
        jnp.where(side[t] == 0, 1 + ranks[t], jnp.where(side[t] < 0, 0, slots + 1)) for t in range(per)
    ]
    late_place = [jnp.maximum(ranks[t] - 1, 0) + jnp.where(side[t] < 0, 0, slots - 1) for t in range(per)]
    early_at = [jnp.clip(at_position(early_place, q), 0, slots + 1) for q in range(per)]
    late_at = [jnp.clip(at_position(late_place, q), 0, 2 * slots - 3) for q in range(per)]
    right_at, left_at = [], []
    for q in range(per):
        right_at.append(sum([jnp.where(order[q] == t - 1, position[t], 0) for t in range(1, per)], jnp.int32(0)))
        left_at.append(sum([jnp.where(order[q] == t + 1, position[t], 0) for t in range(per - 1)], jnp.int32(0)))

    def mix_tile(q, carry):
        t = order[0]
        for i in range(1, per):
            t = jnp.where(q == i, order[i], t)
        for g in range(SIGMAS):
            for h in range(ORDERS):
                p = g * ORDERS + h
                total = coef[t, p * ORDERS] * tab[g * ORDERS]
                for v in range(1, ORDERS):
                    total = total + coef[t, p * ORDERS + v] * tab[g * ORDERS + v]
                mixed[q, pl.ds(p * chunk, chunk), :] = total.astype(BF)
        return carry

    lax.fori_loop(0, per, mix_tile, 0)

    def tiles_arrive(k):
        @pl.when(has_low)
        def _():
            tile_to_high(k, low).wait_recv()

        @pl.when(has_high)
        def _():
            tile_to_low(k, high).wait_recv()

    def down_columns(q, c, at):
        window = pl.ds(pl.multiple_of(c * chunk, chunk), depth)
        result = jnp.dot(mixed[q], ext[q, window, pl.ds(0, tile)], preferred_element_type=F32).astype(BF)
        for p in range(PAIRS):
            column[pl.ds(at * chunk, chunk), pl.ds(p * tile, tile)] = result[p * chunk : (p + 1) * chunk]

    half = per // 2
    tiles_arrive(0)

    def middle(first):
        for q in range(half):
            for i in range(2):
                down_columns(first + q, 1 + i, 2 * q + i)
        result = jnp.dot(column[...], across[...], preferred_element_type=F32)
        for q in range(half):
            matched[first + q, pl.ds(chunk, 2 * chunk), :] = result[2 * q * chunk : 2 * (q + 1) * chunk]

    for q in range(half):
        ext[q, pl.ds(EDGE, tile), pl.ds(0, tile)] = early[early_at[q]]
    middle(0)
    for k in range(1, slots):
        tiles_arrive(k)
    for q in range(half, per):
        x = jnp.where(is_late[q] == 1, late[late_at[q]].astype(F32), early[early_at[q]].astype(F32)).astype(BF)
        ext[q, pl.ds(EDGE, tile), pl.ds(0, tile)] = x

    def halo_to_high(target):
        return remote(halo_out.at[0], halo.at[0], halo_send.at[0], halo_recv.at[0], target)

    def halo_to_low(target):
        return remote(halo_out.at[1], halo.at[1], halo_send.at[1], halo_recv.at[1], target)

    for t in range(per):
        halo_out[0, t] = ext[position[t], pl.ds(tile, EDGE), pl.ds(0, tile)]
        halo_out[1, t] = ext[position[t], pl.ds(EDGE, EDGE), pl.ds(0, tile)]

    @pl.when(has_high)
    def _():
        halo_to_high(high).start()

    @pl.when(has_low)
    def _():
        halo_to_low(low).start()

    def fill_sides(first, count):
        lane = lax.broadcasted_iota(jnp.int32, (count, SIDE), 1)
        none = jnp.zeros((count, SIDE), F32)
        for q in range(per):
            right = ext[right_at[q], pl.ds(first, count), pl.ds(0, SIDE)].astype(F32)
            left = ext[left_at[q], pl.ds(first, count), pl.ds(tile - SIDE, SIDE)].astype(F32)
            right = jnp.where(order[q] + 1 < per, right, none)
            left = jnp.where(order[q] > 0, left, none)
            ext[q, pl.ds(first, count), pl.ds(tile, SIDE)] = jnp.where(lane < SIDE // 2, right, left).astype(BF)

    fill_sides(EDGE, tile)
    middle(half)
    for load in science_loads:
        load.wait()

    def chunk_to_low(k, c, target):
        at = pl.ds(pl.multiple_of(c * chunk, chunk), chunk)
        return remote(
            parcel.at[k, at], out.at[2 * slots + k, at], back_send.at[c, k], back_recv.at[c, k], target
        )

    def chunk_to_high(k, c, target):
        j = slots + k
        at = pl.ds(pl.multiple_of(c * chunk, chunk), chunk)
        return remote(parcel.at[j, at], out.at[k, at], back_send.at[c, j], back_recv.at[c, j], target)

    def position_of(t):
        return sum([jnp.where(t - d * per == s, position[s], 0) for s in range(per)], jnp.int32(0))

    def one_chunk(i, carry):
        c = lax.rem(i + 1, chunks)
        at = pl.ds(pl.multiple_of(c * chunk, chunk), chunk)

        @pl.when(i == chunks - 2)
        def _():
            @pl.when(has_low)
            def _():
                halo_to_high(low).wait_recv()

            @pl.when(has_high)
            def _():
                halo_to_low(high).wait_recv()

            keep_top = has_low & (ccd[d] == 0)
            keep_bottom = has_high & (ccd[jnp.minimum(d + 1, owners - 1)] == 0)
            nothing = jnp.zeros((EDGE, tile), BF)
            for t in range(per):
                top = jnp.where(keep_top, halo[0, order[t]], nothing)
                bottom = jnp.where(keep_bottom, halo[1, order[t]], nothing)
                ext[t, pl.ds(0, EDGE), pl.ds(0, tile)] = top
                ext[t, pl.ds(EDGE + tile, EDGE), pl.ds(0, tile)] = bottom
            fill_sides(0, EDGE)
            fill_sides(EDGE + tile, EDGE)

        @pl.when(i >= chunks - 2)
        def _():
            for q in range(per):
                down_columns(q, c, q)
            result = jnp.dot(column[...], across[...], preferred_element_type=F32)
            for q in range(per):
                matched[q, at, :] = result[q * chunk : (q + 1) * chunk]

        window = pl.ds(pl.multiple_of(c * chunk, chunk), depth)
        for q in range(per):
            result = jnp.dot(
                mixed[q], ext[q, window, pl.ds(tile, SIDE)], preferred_element_type=F32
            ).astype(BF)
            for p in range(PAIRS):
                side_column[pl.ds(q * chunk, chunk), pl.ds(p * SIDE, SIDE)] = result[p * chunk : (p + 1) * chunk]
        sides = jnp.dot(side_column[...], across_side[...], preferred_element_type=F32)
        for q in range(per):
            sky = science[order[q], at, :]
            diff[q, at, :] = (sky - (matched[q, at, :] + sides[q * chunk : (q + 1) * chunk])).astype(BF)
        for k in range(slots):
            parcel[k, at, :] = diff[position_of(from_low[k]), at, :]
            parcel[slots + k, at, :] = diff[position_of(from_high[k]), at, :]

            @pl.when(has_low)
            def _():
                chunk_to_low(k, c, low).start()

            @pl.when(has_high)
            def _():
                chunk_to_high(k, c, high).start()

        return carry

    lax.fori_loop(0, chunks, one_chunk, 0)

    def own_copy(k):
        return pltpu.make_async_copy(back.at[k], out.at[slots + k], out_sem.at[k])

    for k in range(slots):
        t = own_tiles[k]
        back[k] = moved(one_hot(tile, margin[1, t]), diff[position_of(t)], one_hot(tile, -margin[2, t]))
        own_copy(k).start()

    @pl.when(has_low)
    def _():
        for k in range(slots):
            tile_to_low(k, low).wait_send()
            for c in range(chunks):
                chunk_to_low(k, c, low).wait_send()
        halo_to_low(low).wait_send()

    @pl.when(has_high)
    def _():
        for k in range(slots):
            tile_to_high(k, high).wait_send()
            for c in range(chunks):
                chunk_to_high(k, c, high).wait_send()
        halo_to_high(high).wait_send()

    for k in range(slots):
        own_copy(k).wait()

    @pl.when(has_low)
    def _():
        for k in range(slots):
            for c in range(chunks):
                chunk_to_high(k, c, low).wait_recv()

    @pl.when(has_high)
    def _():
        for k in range(slots):
            for c in range(chunks):
                chunk_to_low(k, c, high).wait_recv()


def mean_kernel(
    owners, per, owned, slots,
    margin_h, arrived_h, out_h,
    margin, arrived, nothing, sums, down, right, shifted, load_sem, sems,
):
    d = lax.axis_index("visit")
    tile = nothing.shape[0]
    margin_load = pltpu.make_async_copy(margin_h, margin, load_sem.at[1])
    margin_load.start()
    load = pltpu.make_async_copy(arrived_h, arrived, load_sem.at[0])
    load.start()
    nothing[...] = jnp.zeros(nothing.shape, F32)
    margin_load.wait()
    tiles, ids, there = [], [], []
    for strip in (d - 1, d, d + 1):
        named, local, present = named_tiles(margin, strip, d, owners, per, owned, slots)
        tiles += named
        ids += local
        there += present

    def count_of(p):
        return sum(((ids[j] == p) & (there[j] == 1)).astype(jnp.int32) for j in range(3 * slots))

    def zero(p, carry):
        @pl.when(count_of(p) == 0)
        def _():
            pltpu.make_async_copy(nothing, out_h.at[p], sems.at[p]).start()

        return carry

    lax.fori_loop(0, owned, zero, 0)
    for i, j in enumerate(list(range(slots)) + list(range(2 * slots, 3 * slots))):
        down[i] = one_hot(tile, margin[1, tiles[j]])
        right[i] = one_hot(tile, -margin[2, tiles[j]])
    load.wait()
    for i, j in enumerate(list(range(slots)) + list(range(2 * slots, 3 * slots))):
        shifted[i] = moved(down[i], arrived[j], right[i])

    for j in list(range(slots, 2 * slots)) + list(range(slots)) + list(range(2 * slots, 3 * slots)):
        order = list(range(slots, 2 * slots)) + list(range(slots)) + list(range(2 * slots, 3 * slots))
        at = order.index(j)
        p = ids[j]
        same = [((ids[i] == p) & (there[i] == 1)).astype(jnp.int32) for i in order]
        before = sum(same[:at], jnp.int32(0))
        after = sum(same[at + 1 :], jnp.int32(0))

        @pl.when(there[j] == 1)
        def _():
            x = arrived[j] if slots <= j < 2 * slots else shifted[j if j < slots else j - slots]
            count = jnp.full((1, 1), before + after + 1, jnp.int32).astype(F32)
            value = x.astype(F32) * (1.0 / count)

            @pl.when(before == 0)
            def _():
                sums[p] = value

            @pl.when(before > 0)
            def _():
                sums[p] += value

            @pl.when(after == 0)
            def _():
                pltpu.make_async_copy(sums.at[p], out_h.at[p], sems.at[p]).start()

    def finish(p, carry):
        pltpu.make_async_copy(sums.at[p], out_h.at[p], sems.at[p]).wait()
        return carry

    lax.fori_loop(0, owned, finish, 0)


def body(science, patches, margin, kernel_coef, ccd_first):
    owners = lax.axis_size("visit")
    owned, tile = patches.shape[0], patches.shape[1]
    per = science.shape[1] // tile
    slots = per // 2
    chunks = 4
    chunk = tile // chunks
    depth = chunk + 2 * EDGE
    width = tile + SIDE
    anywhere = pl.BlockSpec(memory_space=pl.ANY)
    hbm = pl.BlockSpec(memory_space=pltpu.HBM)
    dma = pltpu.SemaphoreType.DMA
    margin = margin.T
    arrived = pl.pallas_call(
        functools.partial(match_kernel, owners, per, owned, tile, slots),
        out_shape=jax.ShapeDtypeStruct((3 * slots, tile, tile), BF),
        in_specs=[hbm] * 5,
        out_specs=anywhere,
        scratch_shapes=[
            pltpu.SMEM(margin.shape, jnp.int32),
            pltpu.SMEM(kernel_coef.shape[::-1], F32),
            pltpu.SMEM(ccd_first.shape, jnp.int32),
            pltpu.VMEM((owned, tile, tile), F32),
            pltpu.VMEM((per, tile, tile), F32),
            pltpu.VMEM((2 * slots, tile, tile), BF),
            pltpu.VMEM((slots + 2, tile, tile), BF),
            pltpu.VMEM((2 * slots - 2, tile, tile), BF),
            pltpu.VMEM((per, tile + 2 * EDGE, width), BF),
            pltpu.VMEM((2, per, EDGE, tile), BF),
            pltpu.VMEM((2, per, EDGE, tile), BF),
            pltpu.VMEM((PAIRS, chunk, depth), F32),
            pltpu.VMEM((per, PAIRS * chunk, depth), BF),
            pltpu.VMEM((PAIRS * tile, tile), BF),
            pltpu.VMEM((PAIRS * SIDE, tile), BF),
            pltpu.VMEM((per * chunk, PAIRS * tile), BF),
            pltpu.VMEM((per * chunk, PAIRS * SIDE), BF),
            pltpu.VMEM((per, tile, tile), F32),
            pltpu.VMEM((per, tile, tile), BF),
            pltpu.VMEM((2 * slots, tile, tile), BF),
            pltpu.VMEM((slots, tile, tile), BF),
            dma((4 + per,)),
            dma((2 * slots,)),
            dma((2 * slots,)),
            dma((2,)),
            dma((2,)),
            dma((chunks, 2 * slots)),
            dma((chunks, 2 * slots)),
            dma((slots,)),
        ],
        compiler_params=pltpu.CompilerParams(
            collective_id=0, has_side_effects=True, vmem_limit_bytes=64 * 1024 * 1024 - 3 * slots * tile * tile * 2
        ),
        name="match",
    )(margin, kernel_coef.T, ccd_first, patches, science)
    return pl.pallas_call(
        functools.partial(mean_kernel, owners, per, owned, slots),
        out_shape=jax.ShapeDtypeStruct(patches.shape, F32),
        in_specs=[hbm, anywhere],
        out_specs=hbm,
        scratch_shapes=[
            pltpu.SMEM(margin.shape, jnp.int32),
            pltpu.VMEM(arrived.shape, BF),
            pltpu.VMEM((tile, tile), F32),
            pltpu.VMEM(patches.shape, F32),
            pltpu.VMEM((2 * slots, tile, tile), BF),
            pltpu.VMEM((2 * slots, tile, tile), BF),
            pltpu.VMEM((2 * slots, tile, tile), BF),
            dma((2,)),
            dma((owned,)),
        ],
        compiler_params=pltpu.CompilerParams(vmem_limit_bytes=64 * 1024 * 1024 - 3 * slots * tile * tile * 2),
        name="mean",
    )(margin, arrived)


def solution(mesh):
    in_specs = (
        P(("grp", "visit"), None),
        P(("grp", "visit"), None, None),
        P("grp", None),
        P(None, ("grp", "visit")),
        P("grp"),
    )
    out_specs = P(("grp", "visit"), None, None)
    return jax.shard_map(body, mesh=mesh, in_specs=in_specs, out_specs=out_specs, check_vma=False)
```
